128 devices in a mesh: seq: 16 (over y, z), vocab: 8 (over x, core).
Axes of the slice: x: 4, y: 4, z: 4, core: 2. Of those that a mesh axis runs over, the one named last changes fastest.
Arguments:
- teacher_hidden: bfloat16 [2048, 5120], P('seq', 'vocab'), may hold values from -80 to 80
- teacher_target: int32 [16], P('seq'), may hold values from -1 to 5, as said below
- student_hidden: bfloat16 [2048, 5120], P('seq', 'vocab'), may hold values from -80 to 80
- tile_count: int32 [16], P('seq'), may hold values from 0 to 1, as said below
- response_mask: int32 [2048], P('seq'), may hold values from 0 to 1, as said below
- teacher_head: bfloat16 [5120, 98304], P(None, ('seq', 'vocab')), may hold values from -1 to 1
- student_head: bfloat16 [5120, 98304], P(None, ('seq', 'vocab')), may hold values from -1 to 1
Outputs:
- mean_loss: float32 [], replicated
- student_grad: float32 [2048, 5120], P('seq', 'vocab')
The draws below stay inside these ranges and needn't reach their ends.
Inputs may be any that keep to these rules, and one draw needn't show every extreme that they name: `teacher_target`: each of 0 to 5 appears exactly once, rising along the teacher stream; -1 marks teacher tiles that no response tile takes. `tile_count`: the counts add up to 6. `response_mask`: the first row of every tile is 1.
All inputs are finite; a program needn't handle non-finite values.
Results may differ from the reference program's by a relative error of at most 0.0005.
Values may be sent and summed in bfloat16 or wider, within the bound.
No kernel may reach another device: no remote copies, remote signals or barrier semaphores. Data moves between devices by JAX's collectives and lax.ppermute only.
A program may use at most 128 MiB of HBM per device.

```python
import jax
import jax.numpy as jnp
from jax import lax

D = 5120
TILE = 128
TEA_TILES = 1
STU_TILES = 1
LIVE = 6
VOCAB = 98304
N_SEQ = 16


def live_layout(key):
    key_one, key_two, key_three = jax.random.split(key, 3)
    stu_total = N_SEQ * STU_TILES
    tea_total = N_SEQ * TEA_TILES
    forced = jax.random.randint(key_one, (), 0, N_SEQ)
    rank_list = jax.random.permutation(key_two, stu_total).astype(jnp.int32)
    tile_ids = jnp.arange(stu_total, dtype=jnp.int32)
    shard_of = tile_ids // STU_TILES
    rank_list = jnp.where(shard_of == forced, -1 - tile_ids % STU_TILES, rank_list)
    ordering = jnp.argsort(rank_list, stable=True)
    chosen = jnp.zeros((stu_total,), jnp.int32).at[ordering[:LIVE]].set(1)
    counts = jnp.sum(chosen.reshape(N_SEQ, STU_TILES), axis=1).astype(jnp.int32)
    picked = jax.random.permutation(key_three, tea_total)[:LIVE].astype(jnp.int32)
    in_order = jnp.sort(picked)
    targets = jnp.full((tea_total,), -1, jnp.int32).at[in_order].set(jnp.arange(LIVE, dtype=jnp.int32))
    return (counts, targets)


def draw_tile_count(key, part):
    counts, targets = live_layout(key)
    return counts


def draw_teacher_target(key, part):
    counts, targets = live_layout(key)
    return targets


def draw_response_mask(key, part):
    key = jax.random.fold_in(key, 5)
    row_total = N_SEQ * STU_TILES * TILE
    coins = jax.random.randint(key, (row_total,), 0, 4)
    first_row = jnp.arange(row_total) % TILE == 0
    return jnp.where(first_row, 1, (coins < 3).astype(jnp.int32)).astype(jnp.int32)


def hidden_rows(key, row_total):
    key_one, key_two = jax.random.split(key)
    row_scale = jnp.exp(jax.random.uniform(key_one, (row_total,), jnp.float32, -0.7, 0.47))
    values = jnp.clip(1.5 * jax.random.normal(key_two, (row_total, D), jnp.float32), -9.0, 9.0)
    return (values * row_scale[:, None]).astype(jnp.bfloat16)


def draw_teacher_hidden(key, part):
    key = jax.random.fold_in(key, 7)
    return hidden_rows(key, N_SEQ * TEA_TILES * TILE)


def draw_student_hidden(key, part):
    key = jax.random.fold_in(key, 8)
    return hidden_rows(key, N_SEQ * STU_TILES * TILE)


def head_matrix(key):
    key_one, key_two, key_three = jax.random.split(key, 3)
    column_scale = jnp.exp(jax.random.uniform(key_one, (VOCAB,), jnp.float32, -2.3, 0.0))
    common = jnp.clip(jax.random.normal(key_three, (D,), jnp.float32), -4.0, 4.0) / D ** 0.5
    base = jnp.clip(jax.random.normal(key_two, (D, VOCAB), jnp.float32), -6.0, 6.0)
    return (base * column_scale[None, :] * (1.5 / D ** 0.5) + common[:, None]).astype(jnp.bfloat16)


def draw_teacher_head(key, part):
    key = jax.random.fold_in(key, 11)
    return head_matrix(key)


def draw_student_head(key, part):
    key = jax.random.fold_in(key, 12)
    return head_matrix(key)


def setup_inputs(seed: int = 0) -> dict:
    streams_of = jax.random.split(jax.random.key(seed), 8)
    teacher_hidden = draw_teacher_hidden(jax.random.fold_in(streams_of[7], 71), 0)
    teacher_target = draw_teacher_target(jax.random.fold_in(streams_of[7], 71), 0)
    student_hidden = draw_student_hidden(jax.random.fold_in(streams_of[7], 71), 0)
    tile_count = draw_tile_count(jax.random.fold_in(streams_of[7], 71), 0)
    response_mask = draw_response_mask(jax.random.fold_in(streams_of[7], 71), 0)
    teacher_head = draw_teacher_head(jax.random.fold_in(streams_of[7], 71), 0)
    student_head = draw_student_head(jax.random.fold_in(streams_of[7], 71), 0)
    return dict(teacher_hidden=teacher_hidden, teacher_target=teacher_target, student_hidden=student_hidden, tile_count=tile_count, response_mask=response_mask, teacher_head=teacher_head, student_head=student_head)


loss_scale = 64.0


def reference(teacher_hidden, teacher_target, student_hidden, tile_count, response_mask, teacher_head, student_head):
    highest = lax.Precision.HIGHEST
    slot_ids = jnp.arange(LIVE, dtype=jnp.int32)
    teacher_pick = (teacher_target[None, :] == slot_ids[:, None]).astype(jnp.float32)
    teacher_rows = jnp.dot(teacher_pick, teacher_hidden.astype(jnp.float32).reshape(-1, TILE * D), precision=highest)
    teacher_rows = teacher_rows.astype(jnp.bfloat16).reshape(LIVE, TILE, D)
    start_tile = jnp.cumsum(tile_count) - tile_count
    within = jnp.tile(jnp.arange(STU_TILES, dtype=jnp.int32), N_SEQ)
    slot_of = jnp.where(within < jnp.repeat(tile_count, STU_TILES), jnp.repeat(start_tile, STU_TILES) + within, -1)
    student_pick = (slot_of[None, :] == slot_ids[:, None]).astype(jnp.float32)
    student_rows = jnp.dot(student_pick, student_hidden.astype(jnp.float32).reshape(-1, TILE * D), precision=highest)
    student_rows = student_rows.astype(jnp.bfloat16).reshape(LIVE, TILE, D)
    row_mask = jnp.dot(student_pick, response_mask.astype(jnp.float32).reshape(-1, TILE), precision=highest)
    masked_count = jnp.sum(row_mask)

    def one_tile(packed):
        teach_part, stud_part, mask_part = packed
        teacher_logits = jnp.dot(teach_part, teacher_head, preferred_element_type=jnp.float32)
        student_logits = jnp.dot(stud_part, student_head, preferred_element_type=jnp.float32)
        teacher_log = jax.nn.log_softmax(teacher_logits, axis=1)
        student_log = jax.nn.log_softmax(student_logits, axis=1)
        teacher_prob = jnp.exp(teacher_log)
        row_loss = jnp.sum(teacher_prob * (teacher_log - student_log), axis=1)
        logit_grad = (loss_scale * mask_part)[:, None] * (jnp.exp(student_log) - teacher_prob)
        grad_high = lax.optimization_barrier(logit_grad.astype(jnp.bfloat16))
        grad_low = (logit_grad - grad_high.astype(jnp.float32)).astype(jnp.bfloat16)
        dims = (((1,), (1,)), ((), ()))
        grad_rows = lax.dot_general(grad_high, student_head, dims, preferred_element_type=jnp.float32)
        grad_rows = grad_rows + lax.dot_general(grad_low, student_head, dims, preferred_element_type=jnp.float32)
        return jnp.sum(mask_part * row_loss), grad_rows

    tile_loss, tile_grad = lax.map(one_tile, (teacher_rows, student_rows, row_mask))
    mean_loss = jnp.sum(tile_loss) / masked_count
    student_grad = jnp.dot(student_pick.T, tile_grad.reshape(LIVE, TILE * D), precision=highest)
    return mean_loss, student_grad.reshape(N_SEQ * STU_TILES * TILE, D)
```

```python
import jax
import jax.numpy as jnp
from jax import lax
from jax.sharding import PartitionSpec as P

TILE = 128
LIVE = 6
RING = 4
BOTH = ("seq", "vocab")
loss_scale = 64.0
f32 = jnp.float32
bf16 = jnp.bfloat16


def device_of(y, z, x, c):
    return (y * RING + z) * 2 * RING + x * 2 + c


def fetch(value, axis, step):
    pairs = []
    for y in range(RING):
        for z in range(RING):
            for x in range(RING):
                for c in range(2):
                    at = dict(y=y, z=z, x=x, c=c)
                    here = device_of(**at)
                    at[axis] = (at[axis] + step) % (2 if axis == "c" else RING)
                    pairs.append((device_of(**at), here))
    return lax.ppermute(value, BOTH, pairs)


def in_order(pieces, place, dim):
    size = pieces[0].shape[dim]
    laid = jnp.concatenate(pieces + pieces[:-1], axis=dim)
    first = (RING - place) % RING * size
    return lax.dynamic_slice_in_dim(laid, first, RING * size, dim)


def gather_direct(block, axis, place, dim):
    return in_order([block] + [fetch(block, axis, d) for d in (1, 2, 3)], place, dim)


def gather_ring(block, axis, place, dim):
    ahead, behind = fetch(block, axis, 1), fetch(block, axis, 3)
    far = jnp.concatenate([fetch(ahead[:1], axis, 1), fetch(behind[1:], axis, 3)], axis=0)
    return in_order([block, ahead, far, behind], place, dim)


def chunk(value, place, step, dim):
    size = value.shape[dim] // RING
    return lax.dynamic_slice_in_dim(value, (place + step) % RING * size, size, dim)


def scatter_direct(value, axis, place, dim):
    got = [fetch(chunk(value, place, (RING - d) % RING, dim), axis, d) for d in (1, 2, 3)]
    return chunk(value, place, 0, dim) + got[0] + got[1] + got[2]


def scatter_ring(value, axis, place, dim):
    own, ahead, far, behind = (chunk(value, place, d, dim) for d in range(RING))
    half = own.shape[0] // 2
    from_behind = fetch(far[:half], axis, 3)
    from_ahead = fetch(far[half:], axis, 1)
    ahead = jnp.concatenate([ahead[:half] + from_behind, ahead[half:]], axis=0)
    behind = jnp.concatenate([behind[:half], behind[half:] + from_ahead], axis=0)
    return own + fetch(ahead, axis, 3) + fetch(behind, axis, 1)


def merge(stats):
    t_max, t_sum, s_max, s_sum, gap = ([s[i] for s in stats] for i in range(5))

    def pairwise(terms):
        if len(terms) == 2:
            return terms[0] + terms[1]
        return (terms[0] + terms[2]) + (terms[1] + terms[3])

    def top(terms):
        best = terms[0]
        for t in terms[1:]:
            best = jnp.maximum(best, t)
        return best

    t_top, s_top = top(t_max), top(s_max)
    t_scale = [jnp.exp(m - t_top) for m in t_max]
    s_scale = [jnp.exp(m - s_top) for m in s_max]
    return jnp.stack(
        [
            t_top,
            pairwise([a * b for a, b in zip(t_sum, t_scale)]),
            s_top,
            pairwise([a * b for a, b in zip(s_sum, s_scale)]),
            pairwise([a * b for a, b in zip(gap, t_scale)]),
        ]
    )


def shards(
    teacher_hidden, teacher_target, student_hidden, tile_count, response_mask, teacher_head, student_head
):
    n_seq = lax.axis_size("seq")
    features = teacher_hidden.shape[1]
    share = TILE // n_seq
    seq, voc = lax.axis_index("seq"), lax.axis_index("vocab")
    y, z, x, c = seq // RING, seq % RING, voc // 2, voc % 2

    def halves(head):
        blocks = head.reshape(RING, 2, features, -1)
        keep = lax.dynamic_index_in_dim(blocks, c, 1, keepdims=False)
        give = lax.dynamic_index_in_dim(blocks, 1 - c, 1, keepdims=False)
        return keep.reshape(RING * features, -1), fetch(give.reshape(RING * features, -1), "c", 1)

    t_own, t_par = halves(teacher_head)
    s_own, s_par = halves(student_head)

    rows = jnp.concatenate(
        [teacher_hidden.reshape(n_seq, share, features), student_hidden.reshape(n_seq, share, features)], axis=1
    )
    lists = jnp.concatenate(
        [
            response_mask.astype(bf16)[None],
            jnp.broadcast_to(teacher_target.astype(bf16)[:, None], (1, TILE)),
            jnp.broadcast_to(tile_count.astype(bf16)[:, None], (1, TILE)),
            jnp.zeros((2 * share - 3, TILE), bf16),
        ]
    )
    sent = jnp.concatenate([rows, jnp.broadcast_to(lists[None], (n_seq, 2 * share, TILE))], axis=2)
    got = lax.all_to_all(sent, "seq", 0, 0, tiled=True)
    all_mask = got[:, 0, features:].astype(f32)
    all_target = got[:, 1, features].astype(jnp.int32)
    all_count = got[:, 2, features].astype(jnp.int32)
    slot_ids = jnp.arange(LIVE, dtype=jnp.int32)
    slot_of = jnp.where(all_count > 0, jnp.cumsum(all_count) - all_count, -1)
    t_match = all_target[None, :] == slot_ids[:, None]
    s_match = slot_of[None, :] == slot_ids[:, None]

    def pick(match, tiles):
        return jnp.sum(jnp.where(match[:, :, None, None], tiles[None].astype(f32), 0.0), axis=1).astype(bf16)

    t_rows = pick(t_match, got[:, :share, :features]).reshape(3, 2 * share, features)
    s_rows = pick(s_match, got[:, share:, :features]).reshape(3, 2 * share, features)
    mask = jnp.sum(jnp.where(s_match[:, :, None], all_mask[None], 0.0), axis=1)
    masked_count = jnp.sum(mask)
    mask = mask.reshape(3, 2, RING, RING, share)
    row_mask = jnp.concatenate(
        [
            mask[0].transpose(2, 1, 0, 3).reshape(-1),
            mask[1].transpose(2, 1, 0, 3).reshape(-1),
            mask[2].transpose(1, 2, 0, 3).reshape(-1),
        ]
    )

    part = [jnp.stack([t_rows[p], s_rows[p]]) for p in range(3)]
    part[0] = gather_direct(part[0], "x", x, 2)
    part[1] = gather_direct(part[1], "y", y, 1)
    part[2] = gather_direct(part[2], "z", z, 1)
    part[0] = gather_direct(part[0], "y", y, 1)
    part[1] = gather_direct(part[1], "z", z, 1)
    part[2] = gather_direct(part[2], "x", x, 2)
    part[0] = gather_ring(part[0], "z", z, 1)
    part[1] = gather_ring(part[1], "x", x, 2)
    part[2] = gather_ring(part[2], "y", y, 1)
    t_all = jnp.concatenate([p[0] for p in part], axis=0)
    s_all = jnp.concatenate([p[1] for p in part], axis=0)

    def logits(all_rows, own, par):
        other = fetch(jnp.dot(all_rows, par, preferred_element_type=f32), "c", 1)
        return jnp.dot(all_rows, own, preferred_element_type=f32) + other

    t_logits = logits(t_all, t_own, t_par)
    s_logits = logits(s_all, s_own, s_par)
    t_max, s_max = jnp.max(t_logits, axis=1), jnp.max(s_logits, axis=1)
    t_exp = jnp.exp(t_logits - t_max[:, None])
    s_exp = jnp.exp(s_logits - s_max[:, None])
    stats = jnp.stack(
        [
            t_max,
            jnp.sum(t_exp, axis=1),
            s_max,
            jnp.sum(s_exp, axis=1),
            jnp.sum(t_exp * (t_logits - s_logits), axis=1),
        ]
    )
    stats = merge([stats, fetch(stats, "c", 1)])
    for axis in ("x", "y", "z"):
        stats = merge([stats] + [fetch(stats, axis, d) for d in (1, 2, 3)])
    t_top, t_sum, s_top, s_sum, gap = stats
    row_loss = gap / t_sum - t_top - jnp.log(t_sum) + s_top + jnp.log(s_sum)
    mean_loss = jnp.sum(row_mask * row_loss) / masked_count
    s_factor = loss_scale * row_mask * jnp.exp(s_max - s_top) / s_sum
    t_factor = loss_scale * row_mask * jnp.exp(t_max - t_top) / t_sum
    grad = s_exp * s_factor[:, None] - t_exp * t_factor[:, None]
    high = lax.optimization_barrier(grad.astype(bf16))
    low = (grad - high.astype(f32)).astype(bf16)
    pair = jnp.concatenate([high, low], axis=1)
    pair = jnp.concatenate([pair, fetch(pair, "c", 1)], axis=1)
    head = jnp.concatenate([s_own, s_own, s_par, s_par], axis=1)
    row_grad = lax.dot_general(pair, head, (((1,), (1,)), ((), ())), preferred_element_type=f32)

    third = row_grad.shape[0] // 3
    part = [row_grad[p * third : (p + 1) * third] for p in range(3)]
    part[0] = scatter_ring(part[0], "z", z, 0)
    part[1] = scatter_ring(part[1], "x", x, 1)
    part[2] = scatter_ring(part[2], "y", y, 0)
    part[0] = scatter_direct(part[0], "y", y, 0)
    part[1] = scatter_direct(part[1], "z", z, 0)
    part[2] = scatter_direct(part[2], "x", x, 1)
    part[0] = scatter_direct(part[0], "x", x, 1)
    part[1] = scatter_direct(part[1], "y", y, 0)
    part[2] = scatter_direct(part[2], "z", z, 0)
    summed = jnp.concatenate(part, axis=0).reshape(LIVE, share, features)
    back = jnp.sum(jnp.where(s_match[:, :, None, None], summed[:, None], 0.0), axis=0)
    own_rows = lax.all_to_all(back, "seq", 0, 0, tiled=True)
    return mean_loss, own_rows.reshape(TILE, features)


def solution(mesh):
    return jax.shard_map(
        shards,
        mesh=mesh,
        in_specs=(
            P("seq", "vocab"),
            P("seq"),
            P("seq", "vocab"),
            P("seq"),
            P("seq"),
            P(None, BOTH),
            P(None, BOTH),
        ),
        out_specs=(P(), P("seq", "vocab")),
        check_vma=False,
    )
```

```python
import jax
import jax.numpy as jnp
from jax import lax
from jax.experimental import pallas as pl
from jax.experimental.pallas import tpu as pltpu
from jax.sharding import PartitionSpec as P

TILE = 128
LIVE = 6
RING = 4
BOTH = ("seq", "vocab")
loss_scale = 64.0
VMEM = 24 * 1024 * 1024
f32 = jnp.float32
bf16 = jnp.bfloat16


def device_of(y, z, x, c):
    return (y * RING + z) * 2 * RING + x * 2 + c


def fetch(value, axis, step):
    pairs = []
    for y in range(RING):
        for z in range(RING):
            for x in range(RING):
                for c in range(2):
                    at = dict(y=y, z=z, x=x, c=c)
                    here = device_of(**at)
                    at[axis] = (at[axis] + step) % (2 if axis == "c" else RING)
                    pairs.append((device_of(**at), here))
    return lax.ppermute(value, BOTH, pairs)


def in_order(pieces, place, dim):
    size = pieces[0].shape[dim]
    laid = jnp.concatenate(pieces + pieces[:-1], axis=dim)
    first = (RING - place) % RING * size
    return lax.dynamic_slice_in_dim(laid, first, RING * size, dim)


def gather_direct(block, axis, place, dim):
    return in_order([block] + [fetch(block, axis, d) for d in (1, 2, 3)], place, dim)


def ring_pieces(blocks, axes, half):
    ahead = [fetch(b, a, 1) for b, a in zip(blocks, axes)]
    behind = [fetch(b, a, 3) for b, a in zip(blocks, axes)]
    ahead, behind = lax.optimization_barrier((ahead, behind))
    size = blocks[0].shape[half] // 2
    first = [fetch(lax.slice_in_dim(v, 0, size, axis=half), a, 1) for v, a in zip(ahead, axes)]
    second = [fetch(lax.slice_in_dim(v, size, 2 * size, axis=half), a, 3) for v, a in zip(behind, axes)]
    return list(zip(ahead, first, second, behind))


def chunk(value, place, step, dim):
    size = value.shape[dim] // RING
    return lax.dynamic_slice_in_dim(value, (place + step) % RING * size, size, dim)


def scatter_direct(value, axis, place, dim):
    got = [fetch(chunk(value, place, (RING - d) % RING, dim), axis, d) for d in (1, 2, 3)]
    return chunk(value, place, 0, dim) + got[0] + got[1] + got[2]


def scatter_ring(far, near, axes, half):
    size = far[0].shape[half] // 2
    cut = lambda v, k: lax.slice_in_dim(v, k * size, (k + 1) * size, axis=half)
    from_behind = [fetch(cut(v, 0), a, 3) for v, a in zip(far, axes)]
    from_ahead = [fetch(cut(v, 1), a, 1) for v, a in zip(far, axes)]
    from_behind, from_ahead, near = lax.optimization_barrier((from_behind, from_ahead, near))
    got = []
    for (ahead, behind), b, a, axis in zip(near, from_behind, from_ahead, axes):
        ahead = jnp.concatenate([cut(ahead, 0) + b, cut(ahead, 1)], axis=half)
        behind = jnp.concatenate([cut(behind, 0), cut(behind, 1) + a], axis=half)
        got.append((fetch(ahead, axis, 3), fetch(behind, axis, 1)))
    return got


def merge(stats):
    t_max, t_sum, s_max, s_sum, gap = ([s[i] for s in stats] for i in range(5))

    def pairwise(terms):
        if len(terms) == 2:
            return terms[0] + terms[1]
        return (terms[0] + terms[2]) + (terms[1] + terms[3])

    def top(terms):
        best = terms[0]
        for t in terms[1:]:
            best = jnp.maximum(best, t)
        return best

    t_top, s_top = top(t_max), top(s_max)
    t_scale = [jnp.exp(m - t_top) for m in t_max]
    s_scale = [jnp.exp(m - s_top) for m in s_max]
    return jnp.stack(
        [
            t_top,
            pairwise([a * b for a, b in zip(t_sum, t_scale)]),
            s_top,
            pairwise([a * b for a, b in zip(s_sum, s_scale)]),
            pairwise([a * b for a, b in zip(gap, t_scale)]),
        ]
    )


def times(rows, head):
    return jnp.dot(rows, head, preferred_element_type=f32)


def softmax_rows(place, own, other, part):
    cols = own[0].shape[2]
    inner = 2 * part
    total = RING * RING * inner

    def kernel(place_ref, o_own, o_near, o_far, p_own, p_near, p_far, t_exp, s_exp, stats_ref, table):
        y, z = place_ref[0], place_ref[1]
        lane = lax.broadcasted_iota(jnp.int32, (inner, 128), 1)

        def logit(which, piece, at):
            o, p, base = {
                0: (o_own, p_own, 0),
                1: (o_near, p_near, 0),
                3: (o_near, p_near, RING * inner),
                2: (o_far, p_far, 0),
            }[piece]
            rows = pl.ds(base + at * inner, inner)
            return o[which, rows, :] + p[which, rows, :]

        for dz in range(RING):
            for dy in range(RING):
                t, s = logit(0, dz, dy), logit(1, dy, dz)
                t_max = jnp.max(t, axis=1, keepdims=True)
                s_max = jnp.max(s, axis=1, keepdims=True)
                te, se = jnp.exp(t - t_max), jnp.exp(s - s_max)
                values = [
                    t_max,
                    jnp.sum(te, axis=1, keepdims=True),
                    s_max,
                    jnp.sum(se, axis=1, keepdims=True),
                    jnp.sum(te * (t - s), axis=1, keepdims=True),
                ]
                row = jnp.zeros((inner, 128), f32)
                for i, v in enumerate(values):
                    row = jnp.where(lane == i, v, row)
                ya, za = lax.rem(y + dy, RING), lax.rem(z + dz, RING)
                first = pl.multiple_of((za * RING + ya) * part, 8)
                second = pl.multiple_of(total // 2 + (ya * RING + za) * part, 8)
                for at, lo in ((first, 0), (second, part)):
                    t_exp[pl.ds(at, part), :] = te[lo : lo + part]
                    s_exp[pl.ds(at, part), :] = se[lo : lo + part]
                    table[pl.ds(at, part), :] = row[lo : lo + part]
        stats_ref[...] = jnp.transpose(table[...])[:8]

    vmem = pl.BlockSpec(memory_space=pltpu.VMEM)
    return pl.pallas_call(
        kernel,
        out_shape=(
            jax.ShapeDtypeStruct((total, cols), f32),
            jax.ShapeDtypeStruct((total, cols), f32),
            jax.ShapeDtypeStruct((8, total), f32),
        ),
        in_specs=[pl.BlockSpec(memory_space=pltpu.SMEM)] + [vmem] * 6,
        out_specs=(vmem, vmem, vmem),
        scratch_shapes=[pltpu.VMEM((total, 128), f32)],
        compiler_params=pltpu.CompilerParams(vmem_limit_bytes=VMEM),
        name="softmax_rows",
    )(place, *own, *other)


def split_grad(place, t_exp, s_exp, factors):
    total, cols = t_exp.shape
    rows = total // 2 // RING

    def kernel(place_ref, t_ref, s_ref, factor_ref, own, near, far, table):
        y, z = place_ref[0], place_ref[1]
        table[...] = jnp.transpose(jnp.concatenate([factor_ref[...], jnp.zeros((120, total), f32)]))
        for half, at in ((0, z), (1, y)):
            for step, out, slot in ((0, own, 0), (1, near, 0), (2, far, 0), (3, near, 1)):
                here = pl.multiple_of(half * (total // 2) + lax.rem(at + step, RING) * rows, 8)
                scale = table[pl.ds(here, rows), :]
                grad = s_ref[pl.ds(here, rows), :] * scale[:, 1:2] - t_ref[pl.ds(here, rows), :] * scale[:, 0:1]
                high = grad.astype(bf16)
                low = (grad - high.astype(f32)).astype(bf16)
                to = (half * (2 if out is near else 1) + slot) * rows
                out[0, to : to + rows, :] = high
                out[1, to : to + rows, :] = low

    vmem = pl.BlockSpec(memory_space=pltpu.VMEM)
    shape = lambda n: jax.ShapeDtypeStruct((2, n * rows, cols), bf16)
    return pl.pallas_call(
        kernel,
        out_shape=(shape(2), shape(4), shape(2)),
        in_specs=[pl.BlockSpec(memory_space=pltpu.SMEM)] + [vmem] * 3,
        out_specs=(vmem, vmem, vmem),
        scratch_shapes=[pltpu.VMEM((total, 128), f32)],
        compiler_params=pltpu.CompilerParams(vmem_limit_bytes=VMEM),
        name="split_grad",
    )(place, t_exp, s_exp, factors)


def chunk_grad(own, par, own_head, par_head):
    _, rows, cols = own.shape
    dims = (((1,), (1,)), ((), ()))
    both = lax.dot_general(own.reshape(2 * rows, cols), own_head, dims, preferred_element_type=f32)
    both += lax.dot_general(par.reshape(2 * rows, cols), par_head, dims, preferred_element_type=f32)
    return both[:rows] + both[rows:]


def shards(
    teacher_hidden, teacher_target, student_hidden, tile_count, response_mask, teacher_head, student_head
):
    n_seq = lax.axis_size("seq")
    features = teacher_hidden.shape[1]
    share = TILE // n_seq
    seq, voc = lax.axis_index("seq"), lax.axis_index("vocab")
    y, z, x, c = seq // RING, seq % RING, voc // 2, voc % 2

    parity = c.reshape(1).astype(jnp.int32)
    place = jnp.stack([y, z]).astype(jnp.int32)

    rows = jnp.concatenate(
        [teacher_hidden.reshape(n_seq, share, features), student_hidden.reshape(n_seq, share, features)], axis=1
    )
    lists = jnp.concatenate(
        [
            response_mask.astype(bf16)[None],
            jnp.broadcast_to(teacher_target.astype(bf16)[:, None], (1, TILE)),
            jnp.broadcast_to(tile_count.astype(bf16)[:, None], (1, TILE)),
            jnp.zeros((2 * share - 3, TILE), bf16),
        ]
    )
    sent = jnp.concatenate([rows, jnp.broadcast_to(lists[None], (n_seq, 2 * share, TILE))], axis=2)
    got = lax.all_to_all(sent, "seq", 0, 0, tiled=True)

    def halves(head):
        blocks = head.reshape(RING, 2, features, -1)
        pick = lambda i: lax.dynamic_index_in_dim(blocks, i, 1, keepdims=False).reshape(RING * features, -1)
        return pick(c), pick(1 - c)

    kept, given = zip(*(halves(h) for h in (teacher_head, student_head)))
    got, kept, given = lax.optimization_barrier((got, kept, given))
    t_head, s_head = kept
    t_par, s_par = (fetch(g, "c", 1) for g in given)

    all_mask = got[:, 0, features:].astype(f32)
    all_target = got[:, 1, features].astype(jnp.int32)
    all_count = got[:, 2, features].astype(jnp.int32)
    slot_ids = jnp.arange(LIVE, dtype=jnp.int32)
    slot_of = jnp.where(all_count > 0, jnp.cumsum(all_count) - all_count, -1)
    t_match = all_target[None, :] == slot_ids[:, None]
    s_match = slot_of[None, :] == slot_ids[:, None]

    def pick(match, tiles):
        return jnp.sum(jnp.where(match[:, :, None, None], tiles[None].astype(f32), 0.0), axis=1).astype(bf16)

    t_rows = pick(t_match, got[:, :share, :features]).reshape(LIVE * share, features)
    s_rows = pick(s_match, got[:, share:, :features]).reshape(LIVE * share, features)
    mask = jnp.sum(jnp.where(s_match[:, :, None], all_mask[None], 0.0), axis=1)
    masked_count = jnp.sum(mask)
    part = LIVE // 2 * share
    mask = mask.reshape(2, LIVE // 2, RING, RING, share)
    row_mask = jnp.concatenate(
        [mask[0].transpose(2, 1, 0, 3).reshape(-1), mask[1].transpose(1, 2, 0, 3).reshape(-1)]
    )

    block = gather_direct(jnp.stack([t_rows, s_rows]), "x", x, 2)
    t_block, s_block = block[0], block[1]

    t_ring, s_ring = ring_pieces((t_block, s_block), ("y", "z"), 1)

    def stacked(rows, ring):
        ahead, first, second, behind = ring
        return jnp.concatenate([rows, ahead, jnp.concatenate([first, second], axis=1), behind], axis=0)

    t_own, s_own = lax.optimization_barrier((stacked(t_block, t_ring), stacked(s_block, s_ring)))
    t_ring, s_ring = ring_pieces((t_own, s_own), ("z", "y"), 0)
    pieces = [
        (t_own, s_own),
        tuple(jnp.concatenate([r[0], r[3]]) for r in (t_ring, s_ring)),
        tuple(jnp.concatenate([r[1], r[2]]) for r in (t_ring, s_ring)),
    ]
    mine, other = [], []
    for t_rows, s_rows in pieces:
        other.append(fetch(jnp.stack([times(t_rows, t_par), times(s_rows, s_par)]), "c", 1))
        mine.append(jnp.stack([times(t_rows, t_head), times(s_rows, s_head)]))
    t_exp, s_exp, local = softmax_rows(place, mine, other, part)

    stats = merge([local, fetch(local, "c", 1)])
    for axis in ("x", "y", "z"):
        stats = merge([stats] + [fetch(stats, axis, d) for d in (1, 2, 3)])
    t_top, t_sum, s_top, s_sum, gap = stats
    row_loss = gap / t_sum - t_top - jnp.log(t_sum) + s_top + jnp.log(s_sum)
    mean_loss = jnp.sum(row_mask * row_loss) / masked_count
    t_factor = loss_scale * row_mask * jnp.exp(local[0] - t_top) / t_sum
    s_factor = loss_scale * row_mask * jnp.exp(local[2] - s_top) / s_sum
    factors = jnp.concatenate([t_factor[None], s_factor[None], jnp.zeros((6, t_factor.shape[0]), f32)])
    own, near, far = split_grad(place, t_exp, s_exp, factors)

    far_par, near_par, own_par = fetch(far, "c", 1), fetch(near, "c", 1), fetch(own, "c", 1)
    rows = RING * part
    far = chunk_grad(far, far_par, s_head, s_par)
    near, near_par, far = lax.optimization_barrier((near, near_par, far))
    near = chunk_grad(near, near_par, s_head, s_par)
    own, own_par, near = lax.optimization_barrier((own, own_par, near))
    own = chunk_grad(own, own_par, s_head, s_par)
    cut = lambda v: [v[k * rows : (k + 1) * rows] for k in range(v.shape[0] // rows)]
    far, near, own = cut(far), cut(near), cut(own)
    got = scatter_ring(far, [near[:2], near[2:]], ("z", "y"), 0)
    summed = [o + a + b for o, (a, b) in zip(own, got)]
    chunks = [[chunk(v, p, d, 0) for d in range(RING)] for v, p in zip(summed, (y, z))]
    got = scatter_ring([v[2] for v in chunks], [(v[1], v[3]) for v in chunks], ("y", "z"), 1)
    first, second = (v[0] + a + b for v, (a, b) in zip(chunks, got))
    summed = scatter_direct(jnp.concatenate([first, second], axis=0), "x", x, 1)
    summed = summed.reshape(LIVE, share, features)
    back = jnp.sum(jnp.where(s_match[:, :, None, None], summed[:, None], 0.0), axis=0)
    own_rows = lax.all_to_all(back, "seq", 0, 0, tiled=True)
    return mean_loss, own_rows.reshape(TILE, features)


def solution(mesh):
    return jax.shard_map(
        shards,
        mesh=mesh,
        in_specs=(
            P("seq", "vocab"),
            P("seq"),
            P("seq", "vocab"),
            P("seq"),
            P("seq"),
            P(None, BOTH),
            P(None, BOTH),
        ),
        out_specs=(P(), P("seq", "vocab")),
        check_vma=False,
    )
```

```python
import jax
import jax.numpy as jnp
from jax import lax
from jax.experimental import pallas as pl
from jax.experimental.pallas import tpu as pltpu
from jax.sharding import PartitionSpec as P

TILE = 128
LIVE = 6
RING = 4
BOTH = ("seq", "vocab")
loss_scale = 64.0
VMEM = 20 * 1024 * 1024
f32 = jnp.float32
bf16 = jnp.bfloat16


def device_of(y, z, x, c):
    return (y * RING + z) * 2 * RING + x * 2 + c


def fetch(value, axis, step):
    pairs = []
    for y in range(RING):
        for z in range(RING):
            for x in range(RING):
                for c in range(2):
                    at = dict(y=y, z=z, x=x, c=c)
                    here = device_of(**at)
                    at[axis] = (at[axis] + step) % (2 if axis == "c" else RING)
                    pairs.append((device_of(**at), here))
    return lax.ppermute(value, BOTH, pairs)


def in_order(pieces, place, dim):
    size = pieces[0].shape[dim]
    laid = jnp.concatenate(pieces + pieces[:-1], axis=dim)
    first = (RING - place) % RING * size
    return lax.dynamic_slice_in_dim(laid, first, RING * size, dim)


def gather_direct(block, axis, place, dim):
    return in_order([block] + [fetch(block, axis, d) for d in (1, 2, 3)], place, dim)


def ring_pieces(blocks, axes, half):
    ahead = [fetch(b, a, 1) for b, a in zip(blocks, axes)]
    behind = [fetch(b, a, 3) for b, a in zip(blocks, axes)]
    ahead, behind = lax.optimization_barrier((ahead, behind))
    size = blocks[0].shape[half] // 2
    first = [fetch(lax.slice_in_dim(v, 0, size, axis=half), a, 1) for v, a in zip(ahead, axes)]
    second = [fetch(lax.slice_in_dim(v, size, 2 * size, axis=half), a, 3) for v, a in zip(behind, axes)]
    return list(zip(ahead, first, second, behind))


def chunk(value, place, step, dim):
    size = value.shape[dim] // RING
    return lax.dynamic_slice_in_dim(value, (place + step) % RING * size, size, dim)


def coded(rows):
    top = jnp.max(jnp.abs(rows), axis=1, keepdims=True)
    scale = jnp.clip(jnp.floor(8.0 * jnp.log2(32000.0 / top)), -960.0, 960.0)
    body = jnp.round(rows * jnp.exp2(scale * 0.125)).astype(jnp.int16)
    tag = jnp.broadcast_to(scale, (rows.shape[0], 128)).astype(jnp.int16)
    return jnp.concatenate([body, tag], axis=1)


def decoded(sent):
    width = sent.shape[1] - 128
    scale = sent[:, width : width + 1].astype(f32)
    return sent[:, :width].astype(f32) * jnp.exp2(scale * -0.125)


def scatter_direct(values, axes, places):
    sent = [coded(v) for v in values]
    got = [
        [fetch(chunk(v, p, (RING - d) % RING, 0), a, d) for d in (1, 2, 3)] for v, a, p in zip(sent, axes, places)
    ]
    return [
        chunk(v, p, 0, 0) + decoded(g[0]) + decoded(g[1]) + decoded(g[2]) for v, p, g in zip(values, places, got)
    ]


def scatter_ring(far, near, axes, later):
    size = far[0].shape[0] // 2
    far = [coded(v) for v in far]
    from_behind = [fetch(v[:size], a, 3) for v, a in zip(far, axes)]
    from_ahead = [fetch(v[size:], a, 1) for v, a in zip(far, axes)]
    from_behind, from_ahead, near = lax.optimization_barrier((from_behind, from_ahead, near))
    sent = []
    for (ahead, behind), b, a in zip(near, from_behind, from_ahead):
        ahead = jnp.concatenate([ahead[:size] + decoded(b), ahead[size:]])
        behind = jnp.concatenate([behind[:size], behind[size:] + decoded(a)])
        sent.append((coded(ahead), coded(behind)))
    sent, later = lax.optimization_barrier((sent, later))
    return [(decoded(fetch(f, a, 3)), decoded(fetch(b, a, 1))) for (f, b), a in zip(sent, axes)], later


def merge(stats):
    t_max, t_sum, s_max, s_sum, gap = ([s[i] for s in stats] for i in range(5))

    def pairwise(terms):
        if len(terms) == 2:
            return terms[0] + terms[1]
        return (terms[0] + terms[2]) + (terms[1] + terms[3])

    def top(terms):
        best = terms[0]
        for t in terms[1:]:
            best = jnp.maximum(best, t)
        return best

    t_top, s_top = top(t_max), top(s_max)
    t_scale = [jnp.exp(m - t_top) for m in t_max]
    s_scale = [jnp.exp(m - s_top) for m in s_max]
    return jnp.stack(
        [
            t_top,
            pairwise([a * b for a, b in zip(t_sum, t_scale)]),
            s_top,
            pairwise([a * b for a, b in zip(s_sum, s_scale)]),
            pairwise([a * b for a, b in zip(gap, t_scale)]),
        ]
    )


def times(rows, head):
    return jnp.dot(rows, head, preferred_element_type=f32)


def softmax_rows(place, own, other, part):
    cols = own[0].shape[2]
    inner = 2 * part
    total = RING * RING * inner

    def kernel(place_ref, o_own, o_near, o_far, p_own, p_near, p_far, t_exp, s_exp, stats_ref, table):
        y, z = place_ref[0], place_ref[1]
        lane = lax.broadcasted_iota(jnp.int32, (inner, 128), 1)

        def logit(which, piece, at):
            o, p, base = {
                0: (o_own, p_own, 0),
                1: (o_near, p_near, 0),
                3: (o_near, p_near, RING * inner),
                2: (o_far, p_far, 0),
            }[piece]
            rows = pl.ds(base + at * inner, inner)
            return o[which, rows, :] + p[which, rows, :]

        for dz in range(RING):
            for dy in range(RING):
                t, s = logit(0, dz, dy), logit(1, dy, dz)
                t_max = jnp.max(t, axis=1, keepdims=True)
                s_max = jnp.max(s, axis=1, keepdims=True)
                te, se = jnp.exp(t - t_max), jnp.exp(s - s_max)
                values = [
                    t_max,
                    jnp.sum(te, axis=1, keepdims=True),
                    s_max,
                    jnp.sum(se, axis=1, keepdims=True),
                    jnp.sum(te * (t - s), axis=1, keepdims=True),
                ]
                row = jnp.zeros((inner, 128), f32)
                for i, v in enumerate(values):
                    row = jnp.where(lane == i, v, row)
                ya, za = lax.rem(y + dy, RING), lax.rem(z + dz, RING)
                first = pl.multiple_of((za * RING + ya) * part, 8)
                second = pl.multiple_of(total // 2 + (ya * RING + za) * part, 8)
                for at, lo in ((first, 0), (second, part)):
                    t_exp[pl.ds(at, part), :] = te[lo : lo + part]
                    s_exp[pl.ds(at, part), :] = se[lo : lo + part]
                    table[pl.ds(at, part), :] = row[lo : lo + part]
        stats_ref[...] = jnp.transpose(table[...])[:8]

    vmem = pl.BlockSpec(memory_space=pltpu.VMEM)
    return pl.pallas_call(
        kernel,
        out_shape=(
            jax.ShapeDtypeStruct((total, cols), f32),
            jax.ShapeDtypeStruct((total, cols), f32),
            jax.ShapeDtypeStruct((8, total), f32),
        ),
        in_specs=[pl.BlockSpec(memory_space=pltpu.SMEM)] + [vmem] * 6,
        out_specs=(vmem, vmem, vmem),
        scratch_shapes=[pltpu.VMEM((total, 128), f32)],
        compiler_params=pltpu.CompilerParams(vmem_limit_bytes=VMEM),
        name="softmax_rows",
    )(place, *own, *other)


def split_grad(place, t_exp, s_exp, factors):
    total, cols = t_exp.shape
    rows = total // 2 // RING

    def kernel(place_ref, t_ref, s_ref, factor_ref, own, near, far, table):
        y, z = place_ref[0], place_ref[1]
        table[...] = jnp.transpose(jnp.concatenate([factor_ref[...], jnp.zeros((120, total), f32)]))
        for half, at in ((0, z), (1, y)):
            for step, out, slot in ((0, own, 0), (1, near, 0), (2, far, 0), (3, near, 1)):
                here = pl.multiple_of(half * (total // 2) + lax.rem(at + step, RING) * rows, 8)
                scale = table[pl.ds(here, rows), :]
                grad = s_ref[pl.ds(here, rows), :] * scale[:, 1:2] - t_ref[pl.ds(here, rows), :] * scale[:, 0:1]
                high = grad.astype(bf16)
                low = (grad - high.astype(f32)).astype(bf16)
                to = (half * (2 if out is near else 1) + slot) * rows
                out[0, to : to + rows, :] = high
                out[1, to : to + rows, :] = low

    vmem = pl.BlockSpec(memory_space=pltpu.VMEM)
    shape = lambda n: jax.ShapeDtypeStruct((2, n * rows, cols), bf16)
    return pl.pallas_call(
        kernel,
        out_shape=(shape(2), shape(4), shape(2)),
        in_specs=[pl.BlockSpec(memory_space=pltpu.SMEM)] + [vmem] * 3,
        out_specs=(vmem, vmem, vmem),
        scratch_shapes=[pltpu.VMEM((total, 128), f32)],
        compiler_params=pltpu.CompilerParams(vmem_limit_bytes=VMEM),
        name="split_grad",
    )(place, t_exp, s_exp, factors)


def chunk_grad(own, par, own_head, par_head):
    _, rows, cols = own.shape
    dims = (((1,), (1,)), ((), ()))
    both = lax.dot_general(own.reshape(2 * rows, cols), own_head, dims, preferred_element_type=f32)
    both += lax.dot_general(par.reshape(2 * rows, cols), par_head, dims, preferred_element_type=f32)
    return both[:rows] + both[rows:]


def shards(
    teacher_hidden, teacher_target, student_hidden, tile_count, response_mask, teacher_head, student_head
):
    n_seq = lax.axis_size("seq")
    features = teacher_hidden.shape[1]
    share = TILE // n_seq
    seq, voc = lax.axis_index("seq"), lax.axis_index("vocab")
    y, z, x, c = seq // RING, seq % RING, voc // 2, voc % 2

    parity = c.reshape(1).astype(jnp.int32)
    place = jnp.stack([y, z]).astype(jnp.int32)

    rows = jnp.concatenate(
        [teacher_hidden.reshape(n_seq, share, features), student_hidden.reshape(n_seq, share, features)], axis=1
    )
    lists = jnp.concatenate(
        [
            response_mask.astype(bf16)[None],
            jnp.broadcast_to(teacher_target.astype(bf16)[:, None], (1, TILE)),
            jnp.broadcast_to(tile_count.astype(bf16)[:, None], (1, TILE)),
            jnp.zeros((2 * share - 3, TILE), bf16),
        ]
    )
    sent = jnp.concatenate([rows, jnp.broadcast_to(lists[None], (n_seq, 2 * share, TILE))], axis=2)
    got = lax.all_to_all(sent, "seq", 0, 0, tiled=True)

    def half(head, which):
        blocks = head.reshape(RING, 2, features, -1)
        return lax.dynamic_index_in_dim(blocks, which, 1, keepdims=False).reshape(RING * features, -1)

    kept, given = ([half(h, i) for h in (teacher_head, student_head)] for i in (c, 1 - c))
    got, kept, given = lax.optimization_barrier((got, kept, given))
    t_head, s_head = kept
    t_par, s_par = (fetch(g, "c", 1) for g in given)

    all_mask = got[:, 0, features:].astype(f32)
    all_target = got[:, 1, features].astype(jnp.int32)
    all_count = got[:, 2, features].astype(jnp.int32)
    slot_ids = jnp.arange(LIVE, dtype=jnp.int32)
    slot_of = jnp.where(all_count > 0, jnp.cumsum(all_count) - all_count, -1)
    t_match = all_target[None, :] == slot_ids[:, None]
    s_match = slot_of[None, :] == slot_ids[:, None]

    def pick(match, tiles):
        return jnp.sum(jnp.where(match[:, :, None, None], tiles[None].astype(f32), 0.0), axis=1).astype(bf16)

    t_rows = pick(t_match, got[:, :share, :features]).reshape(LIVE * share, features)
    s_rows = pick(s_match, got[:, share:, :features]).reshape(LIVE * share, features)
    mask = jnp.sum(jnp.where(s_match[:, :, None], all_mask[None], 0.0), axis=1)
    masked_count = jnp.sum(mask)
    part = LIVE // 2 * share
    mask = mask.reshape(2, LIVE // 2, RING, RING, share)
    row_mask = jnp.concatenate(
        [mask[0].transpose(2, 1, 0, 3).reshape(-1), mask[1].transpose(1, 2, 0, 3).reshape(-1)]
    )

    block = gather_direct(jnp.stack([t_rows, s_rows]), "x", x, 2)
    block, t_par, s_par = lax.optimization_barrier((block, t_par, s_par))
    t_block, s_block = block[0], block[1]

    t_ring, s_ring = ring_pieces((t_block, s_block), ("y", "z"), 1)

    def stacked(rows, ring):
        ahead, first, second, behind = ring
        return jnp.concatenate([rows, ahead, jnp.concatenate([first, second], axis=1), behind], axis=0)

    t_own, s_own = stacked(t_block, t_ring), stacked(s_block, s_ring)
    t_own, s_own, row_mask = lax.optimization_barrier((t_own, s_own, row_mask))
    t_ring, s_ring = ring_pieces((t_own, s_own), ("z", "y"), 0)
    t_near, s_near = (jnp.concatenate([r[0], r[3]]) for r in (t_ring, s_ring))
    t_far, s_far = (jnp.concatenate([r[1], r[2]]) for r in (t_ring, s_ring))
    both = lambda t, s: jnp.concatenate([t[None], s[None]])
    other_own, other_near = both(times(t_own, t_par), times(s_own, s_par)), both(times(t_near, t_par), times(s_near, s_par))
    mine_own, mine_near = both(times(t_own, t_head), times(s_own, s_head)), both(times(t_near, t_head), times(s_near, s_head))
    other_own, other_near = fetch(other_own, "c", 1), fetch(other_near, "c", 1)
    t_far, s_far, mine_own, mine_near = lax.optimization_barrier((t_far, s_far, mine_own, mine_near))
    other_far = fetch(both(times(t_far, t_par), times(s_far, s_par)), "c", 1)
    mine_far = both(times(t_far, t_head), times(s_far, s_head))
    mine, other = (mine_own, mine_near, mine_far), (other_own, other_near, other_far)
    t_exp, s_exp, local = softmax_rows(place, mine, other, part)

    stats = merge([local, fetch(local, "c", 1)])
    for axis in ("x", "y", "z"):
        stats = merge([stats] + [fetch(stats, axis, d) for d in (1, 2, 3)])
    t_top, t_sum, s_top, s_sum, gap = stats
    row_loss = gap / t_sum - t_top - jnp.log(t_sum) + s_top + jnp.log(s_sum)
    mean_loss = jnp.sum(row_mask * row_loss) / masked_count
    t_factor = loss_scale * row_mask * jnp.exp(local[0] - t_top) / t_sum
    s_factor = loss_scale * row_mask * jnp.exp(local[2] - s_top) / s_sum
    factors = jnp.concatenate([t_factor[None], s_factor[None], jnp.zeros((6, t_factor.shape[0]), f32)])
    own, near, far = split_grad(place, t_exp, s_exp, factors)

    far_par, near_par, own_par = fetch(far, "c", 1), fetch(near, "c", 1), fetch(own, "c", 1)
    rows = RING * part
    far = chunk_grad(far, far_par, s_head, s_par)
    near, near_par, far = lax.optimization_barrier((near, near_par, far))
    near = chunk_grad(near, near_par, s_head, s_par)
    cut = lambda v: [v[k * rows : (k + 1) * rows] for k in range(v.shape[0] // rows)]
    far, near = cut(far), cut(near)
    got, later = scatter_ring(far, [near[:2], near[2:]], ("z", "y"), (own, own_par))
    own = cut(chunk_grad(*later, s_head, s_par))
    summed = [o + a + b for o, (a, b) in zip(own, got)]
    summed = jnp.concatenate(scatter_direct(summed, ("y", "z"), (y, z)))
    summed = summed.reshape(LIVE * share, RING, features).transpose(1, 0, 2).reshape(RING * LIVE * share, features)
    (summed,) = scatter_direct([summed], ["x"], [x])
    summed = summed.reshape(LIVE, share, features)
    back = jnp.sum(jnp.where(s_match[:, :, None, None], summed[:, None], 0.0), axis=0)
    own_rows = lax.all_to_all(back, "seq", 0, 0, tiled=True)
    return mean_loss, own_rows.reshape(TILE, features)


def solution(mesh):
    return jax.shard_map(
        shards,
        mesh=mesh,
        in_specs=(
            P("seq", "vocab"),
            P("seq"),
            P("seq", "vocab"),
            P("seq"),
            P("seq"),
            P(None, BOTH),
            P(None, BOTH),
        ),
        out_specs=(P(), P("seq", "vocab")),
        check_vma=False,
    )
```

```python
import jax
import jax.numpy as jnp
from jax import lax
from jax.experimental import pallas as pl
from jax.experimental.pallas import tpu as pltpu
from jax.sharding import PartitionSpec as P

TILE = 128
LIVE = 6
RING = 4
BOTH = ("seq", "vocab")
loss_scale = 64.0
VMEM = 20 * 1024 * 1024
f32 = jnp.float32
bf16 = jnp.bfloat16


def device_of(y, z, x, c):
    return (y * RING + z) * 2 * RING + x * 2 + c


def fetch(value, axis, step):
    pairs = []
    for y in range(RING):
        for z in range(RING):
            for x in range(RING):
                for c in range(2):
                    at = dict(y=y, z=z, x=x, c=c)
                    here = device_of(**at)
                    at[axis] = (at[axis] + step) % (2 if axis == "c" else RING)
                    pairs.append((device_of(**at), here))
    return lax.ppermute(value, BOTH, pairs)


def gather_direct(block, axis, first, dim):
    pieces = [block] + [fetch(block, axis, d) for d in (1, 2, 3)]
    laid = jnp.concatenate(pieces + pieces[:-1], axis=dim)
    return lax.dynamic_slice_in_dim(laid, first, RING * block.shape[dim], dim)


def ring_pieces(blocks, axes, half):
    ahead = [fetch(b, a, 1) for b, a in zip(blocks, axes)]
    behind = [fetch(b, a, 3) for b, a in zip(blocks, axes)]
    ahead, behind = lax.optimization_barrier((ahead, behind))
    size = blocks[0].shape[half] // 2
    first = [fetch(lax.slice_in_dim(v, 0, size, axis=half), a, 1) for v, a in zip(ahead, axes)]
    second = [fetch(lax.slice_in_dim(v, size, 2 * size, axis=half), a, 3) for v, a in zip(behind, axes)]
    return list(zip(ahead, first, second, behind))


def chunk(value, starts, step):
    return lax.dynamic_slice_in_dim(value, starts[step], value.shape[0] // RING, 0)


def coded(rows):
    top = jnp.max(jnp.abs(rows), axis=1, keepdims=True)
    scale = jnp.clip(jnp.floor(8.0 * jnp.log2(32000.0 / top)), -960.0, 960.0)
    body = jnp.round(rows * jnp.exp2(scale * 0.125)).astype(jnp.int16)
    tag = jnp.broadcast_to(scale, (rows.shape[0], 128)).astype(jnp.int16)
    return jnp.concatenate([body, tag], axis=1)


def decoded(sent):
    width = sent.shape[1] - 128
    scale = sent[:, width : width + 1].astype(f32)
    return sent[:, :width].astype(f32) * jnp.exp2(scale * -0.125)


def scatter_direct(values, axes, places):
    sent = [coded(v) for v in values]
    got = [
        [fetch(chunk(v, p, (RING - d) % RING), a, d) for d in (1, 2, 3)] for v, a, p in zip(sent, axes, places)
    ]
    return [
        chunk(v, p, 0) + decoded(g[0]) + decoded(g[1]) + decoded(g[2]) for v, p, g in zip(values, places, got)
    ]


def scatter_ring(far, near, axes, later):
    size = far[0].shape[0] // 2
    far = [coded(v) for v in far]
    from_behind = [fetch(v[:size], a, 3) for v, a in zip(far, axes)]
    from_ahead = [fetch(v[size:], a, 1) for v, a in zip(far, axes)]
    from_behind, from_ahead, near = lax.optimization_barrier((from_behind, from_ahead, near))
    sent = []
    for (ahead, behind), b, a in zip(near, from_behind, from_ahead):
        ahead = jnp.concatenate([ahead[:size] + decoded(b), ahead[size:]])
        behind = jnp.concatenate([behind[:size], behind[size:] + decoded(a)])
        sent.append((coded(ahead), coded(behind)))
    sent, later = lax.optimization_barrier((sent, later))
    return [(decoded(fetch(f, a, 3)), decoded(fetch(b, a, 1))) for (f, b), a in zip(sent, axes)], later


def merge(stats, last=None):
    def pairwise(terms):
        if len(terms) == 2:
            return terms[0] + terms[1]
        return (terms[0] + terms[2]) + (terms[1] + terms[3])

    def top(terms):
        best = terms[0]
        for t in terms[1:]:
            best = jnp.maximum(best, t)
        return best

    def kernel(*refs):
        stat_refs, out = refs[: len(stats)], refs[-1]
        t_max, t_sum, s_max, s_sum, gap = ([ref[i : i + 1, :] for ref in stat_refs] for i in range(5))
        t_top, s_top = top(t_max), top(s_max)
        t_scale = [jnp.exp(m - t_top) for m in t_max]
        s_scale = [jnp.exp(m - s_top) for m in s_max]
        t_all = pairwise([a * b for a, b in zip(t_sum, t_scale)])
        s_all = pairwise([a * b for a, b in zip(s_sum, s_scale)])
        gap = pairwise([a * b for a, b in zip(gap, t_scale)])
        rows = [t_top, t_all, s_top, s_all, gap]
        if last:
            local, mask = refs[len(stats)], refs[len(stats) + 1][...]
            rows = [
                loss_scale * mask * jnp.exp(local[0:1, :] - t_top) / t_all,
                loss_scale * mask * jnp.exp(local[2:3, :] - s_top) / s_all,
                mask * (gap / t_all - t_top - jnp.log(t_all) + s_top + jnp.log(s_all)),
            ]
        out[...] = jnp.zeros_like(out)
        for i, row in enumerate(rows):
            out[i : i + 1, :] = row

    operands = [*stats, *(last or ())]
    vmem = pl.BlockSpec(memory_space=pltpu.VMEM)
    return pl.pallas_call(
        kernel,
        out_shape=jax.ShapeDtypeStruct(stats[0].shape, f32),
        in_specs=[vmem] * len(operands),
        out_specs=vmem,
        compiler_params=pltpu.CompilerParams(vmem_limit_bytes=4 * 1024 * 1024),
        name="merge",
    )(*operands)


def times(rows, head):
    return jnp.dot(rows, head, preferred_element_type=f32)


def softmax_rows(place, own, other, part):
    cols = own[0].shape[2]
    inner = 2 * part
    total = RING * RING * inner

    def kernel(place_ref, o_own, o_near, o_far, p_own, p_near, p_far, t_exp, s_exp, stats_ref, table):
        y, z = place_ref[0], place_ref[1]
        lane = lax.broadcasted_iota(jnp.int32, (inner, 128), 1)

        def logit(which, piece, at):
            o, p, base = {
                0: (o_own, p_own, 0),
                1: (o_near, p_near, 0),
                3: (o_near, p_near, RING * inner),
                2: (o_far, p_far, 0),
            }[piece]
            rows = pl.ds(base + at * inner, inner)
            return o[which, rows, :] + p[which, rows, :]

        for dz in range(RING):
            for dy in range(RING):
                t, s = logit(0, dz, dy), logit(1, dy, dz)
                t_max = jnp.max(t, axis=1, keepdims=True)
                s_max = jnp.max(s, axis=1, keepdims=True)
                te, se = jnp.exp(t - t_max), jnp.exp(s - s_max)
                values = [
                    t_max,
                    jnp.sum(te, axis=1, keepdims=True),
                    s_max,
                    jnp.sum(se, axis=1, keepdims=True),
                    jnp.sum(te * (t - s), axis=1, keepdims=True),
                ]
                row = jnp.zeros((inner, 128), f32)
                for i, v in enumerate(values):
                    row = jnp.where(lane == i, v, row)
                ya, za = lax.rem(y + dy, RING), lax.rem(z + dz, RING)
                first = pl.multiple_of((za * RING + ya) * part, 8)
                second = pl.multiple_of(total // 2 + (ya * RING + za) * part, 8)
                for at, lo in ((first, 0), (second, part)):
                    t_exp[pl.ds(at, part), :] = te[lo : lo + part]
                    s_exp[pl.ds(at, part), :] = se[lo : lo + part]
                    table[pl.ds(at, part), :] = row[lo : lo + part]
        stats_ref[...] = jnp.transpose(table[...])[:8]

    vmem = pl.BlockSpec(memory_space=pltpu.VMEM)
    return pl.pallas_call(
        kernel,
        out_shape=(
            jax.ShapeDtypeStruct((total, cols), f32),
            jax.ShapeDtypeStruct((total, cols), f32),
            jax.ShapeDtypeStruct((8, total), f32),
        ),
        in_specs=[pl.BlockSpec(memory_space=pltpu.SMEM)] + [vmem] * 6,
        out_specs=(vmem, vmem, vmem),
        scratch_shapes=[pltpu.VMEM((total, 128), f32)],
        compiler_params=pltpu.CompilerParams(vmem_limit_bytes=VMEM),
        name="softmax_rows",
    )(place, *own, *other)


def split_grad(place, t_exp, s_exp, factors):
    total, cols = t_exp.shape
    rows = total // 2 // RING

    def kernel(place_ref, t_ref, s_ref, factor_ref, own, near, far, table):
        y, z = place_ref[0], place_ref[1]
        table[...] = jnp.transpose(jnp.concatenate([factor_ref[...], jnp.zeros((120, total), f32)]))
        for half, at in ((0, z), (1, y)):
            for step, out, slot in ((0, own, 0), (1, near, 0), (2, far, 0), (3, near, 1)):
                here = pl.multiple_of(half * (total // 2) + lax.rem(at + step, RING) * rows, 8)
                scale = table[pl.ds(here, rows), :]
                grad = s_ref[pl.ds(here, rows), :] * scale[:, 1:2] - t_ref[pl.ds(here, rows), :] * scale[:, 0:1]
                high = grad.astype(bf16)
                low = (grad - high.astype(f32)).astype(bf16)
                to = (half * (2 if out is near else 1) + slot) * rows
                out[0, to : to + rows, :] = high
                out[1, to : to + rows, :] = low

    vmem = pl.BlockSpec(memory_space=pltpu.VMEM)
    shape = lambda n: jax.ShapeDtypeStruct((2, n * rows, cols), bf16)
    return pl.pallas_call(
        kernel,
        out_shape=(shape(2), shape(4), shape(2)),
        in_specs=[pl.BlockSpec(memory_space=pltpu.SMEM)] + [vmem] * 3,
        out_specs=(vmem, vmem, vmem),
        scratch_shapes=[pltpu.VMEM((total, 128), f32)],
        compiler_params=pltpu.CompilerParams(vmem_limit_bytes=VMEM),
        name="split_grad",
    )(place, t_exp, s_exp, factors)


def chunk_grad(own, par, own_head, par_head):
    _, rows, cols = own.shape
    dims = (((1,), (1,)), ((), ()))
    both = lax.dot_general(own.reshape(2 * rows, cols), own_head, dims, preferred_element_type=f32)
    both += lax.dot_general(par.reshape(2 * rows, cols), par_head, dims, preferred_element_type=f32)
    return both[:rows] + both[rows:]


def shards(
    teacher_hidden, teacher_target, student_hidden, tile_count, response_mask, teacher_head, student_head
):
    n_seq = lax.axis_size("seq")
    features = teacher_hidden.shape[1]
    share = TILE // n_seq
    seq, voc = lax.axis_index("seq"), lax.axis_index("vocab")
    y, z, x, c = seq // RING, seq % RING, voc // 2, voc % 2
    part = LIVE // 2 * share
    parity = c.astype(jnp.uint32)
    place = jnp.stack([y, z]).astype(jnp.int32)
    starts = {
        axis: [((at + d) % RING * size).astype(jnp.uint32) for d in range(RING)]
        for axis, at, size in (("y", y, part), ("z", z, part), ("x", x, 2 * part))
    }
    first_x = ((RING - x) % RING * features).astype(jnp.uint32)

    rows = jnp.concatenate(
        [teacher_hidden.reshape(n_seq, share, features), student_hidden.reshape(n_seq, share, features)], axis=1
    )
    lists = jnp.concatenate(
        [
            response_mask.astype(bf16)[None],
            jnp.broadcast_to(teacher_target.astype(bf16)[:, None], (1, TILE)),
            jnp.broadcast_to(tile_count.astype(bf16)[:, None], (1, TILE)),
            jnp.zeros((2 * share - 3, TILE), bf16),
        ]
    )
    sent = jnp.concatenate([rows, jnp.broadcast_to(lists[None], (n_seq, 2 * share, TILE))], axis=2)
    sent, parity, place, starts, first_x = lax.optimization_barrier((sent, parity, place, starts, first_x))
    got = lax.all_to_all(sent, "seq", 0, 0, tiled=True)

    def half(head, which):
        blocks = head.reshape(RING, 2, features, -1)
        return lax.dynamic_index_in_dim(blocks, which, 1, keepdims=False).reshape(RING * features, -1)

    kept, given = ([half(h, i) for h in (teacher_head, student_head)] for i in (parity, 1 - parity))
    got, kept, given = lax.optimization_barrier((got, kept, given))
    t_head, s_head = kept
    all_mask = got[:, 0, features:].astype(f32)
    all_target = got[:, 1, features].astype(jnp.int32)
    all_count = got[:, 2, features].astype(jnp.int32)
    slot_ids = jnp.arange(LIVE, dtype=jnp.int32)
    tiles = jnp.arange(n_seq, dtype=jnp.int32)
    before = jnp.sum(jnp.where(tiles[None, :] < tiles[:, None], all_count[None, :], 0), axis=1)
    slot_of = jnp.where(all_count > 0, before, -1)
    t_match = all_target[None, :] == slot_ids[:, None]
    s_match = slot_of[None, :] == slot_ids[:, None]

    def pick(match, tiles):
        return jnp.sum(jnp.where(match[:, :, None, None], tiles[None].astype(f32), 0.0), axis=1).astype(bf16)

    t_rows = pick(t_match, got[:, :share, :features]).reshape(LIVE * share, features)
    s_rows = pick(s_match, got[:, share:, :features]).reshape(LIVE * share, features)
    mask = jnp.sum(jnp.where(s_match[:, :, None], all_mask[None], 0.0), axis=1)
    masked_count = jnp.sum(mask)
    mask = mask.reshape(2, LIVE // 2, RING, RING, share)
    row_mask = jnp.concatenate(
        [mask[0].transpose(2, 1, 0, 3).reshape(-1), mask[1].transpose(1, 2, 0, 3).reshape(-1)]
    )

    row_mask = row_mask.reshape(1, -1)
    given, row_mask, masked_count = lax.optimization_barrier((given, row_mask, masked_count))
    t_par, s_par = (fetch(g, "c", 1) for g in given)

    block = gather_direct(jnp.stack([t_rows, s_rows]), "x", first_x, 2)
    block, t_par, s_par = lax.optimization_barrier((block, t_par, s_par))
    t_block, s_block = block[0], block[1]

    t_ring, s_ring = ring_pieces((t_block, s_block), ("y", "z"), 1)

    def stacked(rows, ring):
        ahead, first, second, behind = ring
        return jnp.concatenate([rows, ahead, jnp.concatenate([first, second], axis=1), behind], axis=0)

    t_own, s_own = stacked(t_block, t_ring), stacked(s_block, s_ring)
    t_own, s_own = lax.optimization_barrier((t_own, s_own))
    t_ring, s_ring = ring_pieces((t_own, s_own), ("z", "y"), 0)
    t_near, s_near = (jnp.concatenate([r[0], r[3]]) for r in (t_ring, s_ring))
    t_far, s_far = (jnp.concatenate([r[1], r[2]]) for r in (t_ring, s_ring))
    both = lambda t, s: jnp.concatenate([t[None], s[None]])
    other_own, other_near = both(times(t_own, t_par), times(s_own, s_par)), both(times(t_near, t_par), times(s_near, s_par))
    mine_own, mine_near = both(times(t_own, t_head), times(s_own, s_head)), both(times(t_near, t_head), times(s_near, s_head))
    other_own, other_near = fetch(other_own, "c", 1), fetch(other_near, "c", 1)
    t_far, s_far, mine_own, mine_near = lax.optimization_barrier((t_far, s_far, mine_own, mine_near))
    other_far = fetch(both(times(t_far, t_par), times(s_far, s_par)), "c", 1)
    mine_far = both(times(t_far, t_head), times(s_far, s_head))
    mine, other = (mine_own, mine_near, mine_far), (other_own, other_near, other_far)
    t_exp, s_exp, local = softmax_rows(place, mine, other, part)

    stats = merge([local, fetch(local, "c", 1)])
    for axis in ("x", "y", "z"):
        stats = merge(
            [stats] + [fetch(stats, axis, d) for d in (1, 2, 3)], (local, row_mask) if axis == "z" else None
        )
    factors = stats
    mean_loss = jnp.sum(stats[2]) / masked_count
    own, near, far = split_grad(place, t_exp, s_exp, factors)

    far_par, near_par, own_par = fetch(far, "c", 1), fetch(near, "c", 1), fetch(own, "c", 1)
    rows = RING * part
    far = chunk_grad(far, far_par, s_head, s_par)
    near, near_par, far = lax.optimization_barrier((near, near_par, far))
    near = chunk_grad(near, near_par, s_head, s_par)
    cut = lambda v: [v[k * rows : (k + 1) * rows] for k in range(v.shape[0] // rows)]
    far, near = cut(far), cut(near)
    got, later = scatter_ring(far, [near[:2], near[2:]], ("z", "y"), (own, own_par))
    own = cut(chunk_grad(*later, s_head, s_par))
    summed = [o + a + b for o, (a, b) in zip(own, got)]
    summed = jnp.concatenate(scatter_direct(summed, ("y", "z"), (starts["y"], starts["z"])))
    summed = summed.reshape(LIVE * share, RING, features).transpose(1, 0, 2).reshape(RING * LIVE * share, features)
    (summed,) = scatter_direct([summed], ["x"], [starts["x"]])
    summed = summed.reshape(LIVE, share, features)
    back = jnp.sum(jnp.where(s_match[:, :, None, None], summed[:, None], 0.0), axis=0)
    own_rows = lax.all_to_all(back, "seq", 0, 0, tiled=True)
    return mean_loss, own_rows.reshape(TILE, features)


def solution(mesh):
    return jax.shard_map(
        shards,
        mesh=mesh,
        in_specs=(
            P("seq", "vocab"),
            P("seq"),
            P("seq", "vocab"),
            P("seq"),
            P("seq"),
            P(None, BOTH),
            P(None, BOTH),
        ),
        out_specs=(P(), P("seq", "vocab")),
        check_vma=False,
    )
```

```python
import jax
import jax.numpy as jnp
from jax import lax
from jax.experimental import pallas as pl
from jax.experimental.pallas import tpu as pltpu
from jax.sharding import PartitionSpec as P

TILE = 128
LIVE = 6
RING = 4
BOTH = ("seq", "vocab")
loss_scale = 64.0
VMEM = 20 * 1024 * 1024
f32 = jnp.float32
bf16 = jnp.bfloat16


def device_of(y, z, x, c):
    return (y * RING + z) * 2 * RING + x * 2 + c


def fetch(value, axis, step):
    pairs = []
    for y in range(RING):
        for z in range(RING):
            for x in range(RING):
                for c in range(2):
                    at = dict(y=y, z=z, x=x, c=c)
                    here = device_of(**at)
                    at[axis] = (at[axis] + step) % (2 if axis == "c" else RING)
                    pairs.append((device_of(**at), here))
    return lax.ppermute(value, BOTH, pairs)


def gather_direct(block, axis, first, dim):
    pieces = [block] + [fetch(block, axis, d) for d in (1, 2, 3)]
    laid = jnp.concatenate(pieces + pieces[:-1], axis=dim)
    return lax.dynamic_slice_in_dim(laid, first, RING * block.shape[dim], dim)


def ring_pieces(blocks, axes, half):
    ahead = [fetch(b, a, 1) for b, a in zip(blocks, axes)]
    behind = [fetch(b, a, 3) for b, a in zip(blocks, axes)]
    ahead, behind = lax.optimization_barrier((ahead, behind))
    size = blocks[0].shape[half] // 2
    first = [fetch(lax.slice_in_dim(v, 0, size, axis=half), a, 1) for v, a in zip(ahead, axes)]
    second = [fetch(lax.slice_in_dim(v, size, 2 * size, axis=half), a, 3) for v, a in zip(behind, axes)]
    return list(zip(ahead, first, second, behind))


def chunk(value, starts, step):
    return lax.dynamic_slice_in_dim(value, starts[step], value.shape[0] // RING, 0)


def coded(rows):
    top = jnp.max(jnp.abs(rows), axis=1, keepdims=True)
    scale = jnp.clip(jnp.floor(8.0 * jnp.log2(32000.0 / top)), -960.0, 960.0)
    body = jnp.round(rows * jnp.exp2(scale * 0.125)).astype(jnp.int16)
    tag = jnp.broadcast_to(scale, (rows.shape[0], 128)).astype(jnp.int16)
    return jnp.concatenate([body, tag], axis=1)


def decoded(sent):
    width = sent.shape[1] - 128
    scale = sent[:, width : width + 1].astype(f32)
    return sent[:, :width].astype(f32) * jnp.exp2(scale * -0.125)


def scatter_direct(values, axes, places):
    sent = [coded(v) for v in values]
    got = [
        [fetch(chunk(v, p, (RING - d) % RING), a, d) for d in (1, 2, 3)] for v, a, p in zip(sent, axes, places)
    ]
    return [
        chunk(v, p, 0) + decoded(g[0]) + decoded(g[1]) + decoded(g[2]) for v, p, g in zip(values, places, got)
    ]


def scatter_ring(far, near, axes, later):
    size = far[0].shape[0] // 2
    far = [coded(v) for v in far]
    from_behind = [fetch(v[:size], a, 3) for v, a in zip(far, axes)]
    from_ahead = [fetch(v[size:], a, 1) for v, a in zip(far, axes)]
    from_behind, from_ahead, near = lax.optimization_barrier((from_behind, from_ahead, near))
    sent = []
    for (ahead, behind), b, a in zip(near, from_behind, from_ahead):
        ahead = jnp.concatenate([ahead[:size] + decoded(b), ahead[size:]])
        behind = jnp.concatenate([behind[:size], behind[size:] + decoded(a)])
        sent.append((coded(ahead), coded(behind)))
    sent, later = lax.optimization_barrier((sent, later))
    return [(decoded(fetch(f, a, 3)), decoded(fetch(b, a, 1))) for (f, b), a in zip(sent, axes)], later


def merge(stats, last=None):
    def pairwise(terms):
        if len(terms) == 2:
            return terms[0] + terms[1]
        return (terms[0] + terms[2]) + (terms[1] + terms[3])

    def top(terms):
        best = terms[0]
        for t in terms[1:]:
            best = jnp.maximum(best, t)
        return best

    def kernel(*refs):
        stat_refs, out = refs[: len(stats)], refs[-1]
        t_max, t_sum, s_max, s_sum, gap = ([ref[i : i + 1, :] for ref in stat_refs] for i in range(5))
        t_top, s_top = top(t_max), top(s_max)
        t_scale = [jnp.exp(m - t_top) for m in t_max]
        s_scale = [jnp.exp(m - s_top) for m in s_max]
        t_all = pairwise([a * b for a, b in zip(t_sum, t_scale)])
        s_all = pairwise([a * b for a, b in zip(s_sum, s_scale)])
        gap = pairwise([a * b for a, b in zip(gap, t_scale)])
        rows = [t_top, t_all, s_top, s_all, gap]
        if last:
            local, mask = refs[len(stats)], refs[len(stats) + 1][...]
            rows = [
                loss_scale * mask * jnp.exp(local[0:1, :] - t_top) / t_all,
                loss_scale * mask * jnp.exp(local[2:3, :] - s_top) / s_all,
                mask * (gap / t_all - t_top - jnp.log(t_all) + s_top + jnp.log(s_all)),
            ]
        out[...] = jnp.zeros_like(out)
        for i, row in enumerate(rows):
            out[i : i + 1, :] = row

    operands = [*stats, *(last or ())]
    vmem = pl.BlockSpec(memory_space=pltpu.VMEM)
    return pl.pallas_call(
        kernel,
        out_shape=jax.ShapeDtypeStruct(stats[0].shape, f32),
        in_specs=[vmem] * len(operands),
        out_specs=vmem,
        compiler_params=pltpu.CompilerParams(vmem_limit_bytes=4 * 1024 * 1024),
        name="merge",
    )(*operands)


def times(rows, head):
    return jnp.dot(rows, head, preferred_element_type=f32)


def softmax_rows(place, own, other, part):
    cols = own[0].shape[2]
    inner = 2 * part
    total = RING * RING * inner

    def kernel(place_ref, o_own, o_near, o_far, p_own, p_near, p_far, t_exp, s_exp, stats_ref, table):
        y, z = place_ref[0], place_ref[1]
        lane = lax.broadcasted_iota(jnp.int32, (inner, 128), 1)

        def logit(which, piece, at):
            o, p, base = {
                0: (o_own, p_own, 0),
                1: (o_near, p_near, 0),
                3: (o_near, p_near, RING * inner),
                2: (o_far, p_far, 0),
            }[piece]
            rows = pl.ds(base + at * inner, inner)
            return o[which, rows, :] + p[which, rows, :]

        for dz in range(RING):
            for dy in range(RING):
                t, s = logit(0, dz, dy), logit(1, dy, dz)
                t_max = jnp.max(t, axis=1, keepdims=True)
                s_max = jnp.max(s, axis=1, keepdims=True)
                te, se = jnp.exp(t - t_max), jnp.exp(s - s_max)
                values = [
                    t_max,
                    jnp.sum(te, axis=1, keepdims=True),
                    s_max,
                    jnp.sum(se, axis=1, keepdims=True),
                    jnp.sum(te * (t - s), axis=1, keepdims=True),
                ]
                row = jnp.zeros((inner, 128), f32)
                for i, v in enumerate(values):
                    row = jnp.where(lane == i, v, row)
                ya, za = lax.rem(y + dy, RING), lax.rem(z + dz, RING)
                first = pl.multiple_of((za * RING + ya) * part, 8)
                second = pl.multiple_of(total // 2 + (ya * RING + za) * part, 8)
                for at, lo in ((first, 0), (second, part)):
                    t_exp[pl.ds(at, part), :] = te[lo : lo + part]
                    s_exp[pl.ds(at, part), :] = se[lo : lo + part]
                    table[pl.ds(at, part), :] = row[lo : lo + part]
        stats_ref[...] = jnp.transpose(table[...])[:8]

    vmem = pl.BlockSpec(memory_space=pltpu.VMEM)
    return pl.pallas_call(
        kernel,
        out_shape=(
            jax.ShapeDtypeStruct((total, cols), f32),
            jax.ShapeDtypeStruct((total, cols), f32),
            jax.ShapeDtypeStruct((8, total), f32),
        ),
        in_specs=[pl.BlockSpec(memory_space=pltpu.SMEM)] + [vmem] * 6,
        out_specs=(vmem, vmem, vmem),
        scratch_shapes=[pltpu.VMEM((total, 128), f32)],
        compiler_params=pltpu.CompilerParams(vmem_limit_bytes=VMEM),
        name="softmax_rows",
    )(place, *own, *other)


def split_grad(place, t_exp, s_exp, factors):
    total, cols = t_exp.shape
    rows = total // 2 // RING

    def kernel(place_ref, t_ref, s_ref, factor_ref, own, near_z, near_y, far, table):
        y, z = place_ref[0], place_ref[1]
        table[...] = jnp.transpose(jnp.concatenate([factor_ref[...], jnp.zeros((120, total), f32)]))
        for half, at, near in ((0, z, near_z), (1, y, near_y)):
            for step, out, slot in ((0, own, half), (1, near, 0), (2, far, half), (3, near, 1)):
                here = pl.multiple_of(half * (total // 2) + lax.rem(at + step, RING) * rows, 8)
                scale = table[pl.ds(here, rows), :]
                grad = s_ref[pl.ds(here, rows), :] * scale[:, 1:2] - t_ref[pl.ds(here, rows), :] * scale[:, 0:1]
                high = grad.astype(bf16)
                low = (grad - high.astype(f32)).astype(bf16)
                to = slot * rows
                out[0, to : to + rows, :] = high
                out[1, to : to + rows, :] = low

    vmem = pl.BlockSpec(memory_space=pltpu.VMEM)
    shape = jax.ShapeDtypeStruct((2, 2 * rows, cols), bf16)
    return pl.pallas_call(
        kernel,
        out_shape=(shape,) * 4,
        in_specs=[pl.BlockSpec(memory_space=pltpu.SMEM)] + [vmem] * 3,
        out_specs=(vmem,) * 4,
        scratch_shapes=[pltpu.VMEM((total, 128), f32)],
        compiler_params=pltpu.CompilerParams(vmem_limit_bytes=VMEM),
        name="split_grad",
    )(place, t_exp, s_exp, factors)


def chunk_grad(own, par, own_head, par_head):
    _, rows, cols = own.shape
    dims = (((1,), (1,)), ((), ()))
    both = lax.dot_general(own.reshape(2 * rows, cols), own_head, dims, preferred_element_type=f32)
    both += lax.dot_general(par.reshape(2 * rows, cols), par_head, dims, preferred_element_type=f32)
    return both[:rows] + both[rows:]


def shards(
    teacher_hidden, teacher_target, student_hidden, tile_count, response_mask, teacher_head, student_head
):
    n_seq = lax.axis_size("seq")
    features = teacher_hidden.shape[1]
    share = TILE // n_seq
    seq, voc = lax.axis_index("seq"), lax.axis_index("vocab")
    y, z, x, c = seq // RING, seq % RING, voc // 2, voc % 2
    part = LIVE // 2 * share
    parity = c.astype(jnp.uint32)
    place = jnp.stack([y, z]).astype(jnp.int32)
    starts = {
        axis: [((at + d) % RING * size).astype(jnp.uint32) for d in range(RING)]
        for axis, at, size in (("y", y, part), ("z", z, part), ("x", x, 2 * part))
    }
    first_x = ((RING - x) % RING * features).astype(jnp.uint32)

    rows = jnp.concatenate(
        [teacher_hidden.reshape(n_seq, share, features), student_hidden.reshape(n_seq, share, features)], axis=1
    )
    lists = jnp.concatenate(
        [
            response_mask.astype(bf16)[None],
            jnp.broadcast_to(teacher_target.astype(bf16)[:, None], (1, TILE)),
            jnp.broadcast_to(tile_count.astype(bf16)[:, None], (1, TILE)),
            jnp.zeros((2 * share - 3, TILE), bf16),
        ]
    )
    sent = jnp.concatenate([rows, jnp.broadcast_to(lists[None], (n_seq, 2 * share, TILE))], axis=2)
    sent, parity, place, starts, first_x = lax.optimization_barrier((sent, parity, place, starts, first_x))
    got = lax.all_to_all(sent, "seq", 0, 0, tiled=True)

    def half(head, which):
        blocks = head.reshape(RING, 2, features, -1)
        return lax.dynamic_index_in_dim(blocks, which, 1, keepdims=False).reshape(RING * features, -1)

    kept, given = ([half(h, i) for h in (teacher_head, student_head)] for i in (parity, 1 - parity))
    got, kept, given = lax.optimization_barrier((got, kept, given))
    t_head, s_head = kept
    all_mask = got[:, 0, features:].astype(f32)
    all_target = got[:, 1, features].astype(jnp.int32)
    all_count = got[:, 2, features].astype(jnp.int32)
    slot_ids = jnp.arange(LIVE, dtype=jnp.int32)
    tiles = jnp.arange(n_seq, dtype=jnp.int32)
    before = jnp.sum(jnp.where(tiles[None, :] < tiles[:, None], all_count[None, :], 0), axis=1)
    slot_of = jnp.where(all_count > 0, before, -1)
    t_match = all_target[None, :] == slot_ids[:, None]
    s_match = slot_of[None, :] == slot_ids[:, None]

    def pick(match, tiles):
        return jnp.sum(jnp.where(match[:, :, None, None], tiles[None].astype(f32), 0.0), axis=1).astype(bf16)

    t_rows = pick(t_match, got[:, :share, :features]).reshape(LIVE * share, features)
    s_rows = pick(s_match, got[:, share:, :features]).reshape(LIVE * share, features)
    mask = jnp.sum(jnp.where(s_match[:, :, None], all_mask[None], 0.0), axis=1)
    masked_count = jnp.sum(mask)
    row = lax.broadcasted_iota(jnp.int32, (TILE, LIVE * TILE), 0)
    col = lax.broadcasted_iota(jnp.int32, (TILE, LIVE * TILE), 1)
    outer, inner = col % (LIVE // 2 * TILE) // (RING * part), col % (RING * part) // part
    second = col >= LIVE // 2 * TILE
    wanted = jnp.where(second, outer * RING + inner, inner * RING + outer) * share + col % share
    spread = jnp.dot(mask.astype(bf16), (row == wanted).astype(bf16), preferred_element_type=f32)
    tile = (col % part // share + jnp.where(second, LIVE // 2, 0))[:LIVE]
    row_mask = jnp.sum(jnp.where(tile == row[:LIVE], spread, 0.0), axis=0, keepdims=True)
    t_par, s_par = (fetch(g, "c", 1) for g in given)

    block = gather_direct(jnp.stack([t_rows, s_rows]), "x", first_x, 2)
    block, t_par, s_par = lax.optimization_barrier((block, t_par, s_par))
    t_block, s_block = block[0], block[1]

    t_ring, s_ring = ring_pieces((t_block, s_block), ("y", "z"), 1)

    def stacked(rows, ring):
        ahead, first, second, behind = ring
        return jnp.concatenate([rows, ahead, jnp.concatenate([first, second], axis=1), behind], axis=0)

    t_own, s_own = stacked(t_block, t_ring), stacked(s_block, s_ring)
    t_own, s_own = lax.optimization_barrier((t_own, s_own))
    t_ring, s_ring = ring_pieces((t_own, s_own), ("z", "y"), 0)
    t_near, s_near = (jnp.concatenate([r[0], r[3]]) for r in (t_ring, s_ring))
    t_far, s_far = (jnp.concatenate([r[1], r[2]]) for r in (t_ring, s_ring))
    both = lambda t, s: jnp.concatenate([t[None], s[None]])
    other_own, other_near = both(times(t_own, t_par), times(s_own, s_par)), both(times(t_near, t_par), times(s_near, s_par))
    mine_own, mine_near = both(times(t_own, t_head), times(s_own, s_head)), both(times(t_near, t_head), times(s_near, s_head))
    other_own, other_near = fetch(other_own, "c", 1), fetch(other_near, "c", 1)
    t_far, s_far, mine_own, mine_near = lax.optimization_barrier((t_far, s_far, mine_own, mine_near))
    other_far = fetch(both(times(t_far, t_par), times(s_far, s_par)), "c", 1)
    mine_far = both(times(t_far, t_head), times(s_far, s_head))
    mine, other = (mine_own, mine_near, mine_far), (other_own, other_near, other_far)
    t_exp, s_exp, local = softmax_rows(place, mine, other, part)

    stats = merge([local, fetch(local, "c", 1)])
    for axis in ("x", "y", "z"):
        stats = merge(
            [stats] + [fetch(stats, axis, d) for d in (1, 2, 3)], (local, row_mask) if axis == "z" else None
        )
    factors = stats
    mean_loss = jnp.sum(stats[2]) / masked_count
    own, near_z, near_y, far = split_grad(place, t_exp, s_exp, factors)

    far_par, near_z_par, near_y_par, own_par = (fetch(v, "c", 1) for v in (far, near_z, near_y, own))
    rows = RING * part
    far = chunk_grad(far, far_par, s_head, s_par)
    near_z, near_z_par, near_y, near_y_par, far = lax.optimization_barrier((near_z, near_z_par, near_y, near_y_par, far))
    near_z = chunk_grad(near_z, near_z_par, s_head, s_par)
    near_y = chunk_grad(near_y, near_y_par, s_head, s_par)
    cut = lambda v: [v[:rows], v[rows:]]
    got, later = scatter_ring(cut(far), [cut(near_z), cut(near_y)], ("z", "y"), (own, own_par))
    own = cut(chunk_grad(*later, s_head, s_par))
    summed = [o + a + b for o, (a, b) in zip(own, got)]
    summed = jnp.concatenate(scatter_direct(summed, ("y", "z"), (starts["y"], starts["z"])))
    summed = summed.reshape(LIVE * share, RING, features).transpose(1, 0, 2).reshape(RING * LIVE * share, features)
    (summed,) = scatter_direct([summed], ["x"], [starts["x"]])
    summed = summed.reshape(LIVE, share, features)
    back = jnp.sum(jnp.where(s_match[:, :, None, None], summed[:, None], 0.0), axis=0)
    own_rows = lax.all_to_all(back, "seq", 0, 0, tiled=True)
    return mean_loss, own_rows.reshape(TILE, features)


def solution(mesh):
    return jax.shard_map(
        shards,
        mesh=mesh,
        in_specs=(
            P("seq", "vocab"),
            P("seq"),
            P("seq", "vocab"),
            P("seq"),
            P("seq"),
            P(None, BOTH),
            P(None, BOTH),
        ),
        out_specs=(P(), P("seq", "vocab")),
        check_vma=False,
    )
```

```python
import jax
import jax.numpy as jnp
from jax import lax
from jax.experimental import pallas as pl
from jax.experimental.pallas import tpu as pltpu
from jax.sharding import PartitionSpec as P

TILE = 128
LIVE = 6
RING = 4
BOTH = ("seq", "vocab")
loss_scale = 64.0
VMEM = 20 * 1024 * 1024
f32 = jnp.float32
bf16 = jnp.bfloat16


def device_of(y, z, x, c):
    return (y * RING + z) * 2 * RING + x * 2 + c


def fetch(value, axis, step):
    pairs = []
    for y in range(RING):
        for z in range(RING):
            for x in range(RING):
                for c in range(2):
                    at = dict(y=y, z=z, x=x, c=c)
                    here = device_of(**at)
                    at[axis] = (at[axis] + step) % (2 if axis == "c" else RING)
                    pairs.append((device_of(**at), here))
    return lax.ppermute(value, BOTH, pairs)


def gather_direct(block, axis, first, dim):
    pieces = [block] + [fetch(block, axis, d) for d in (1, 2, 3)]
    laid = jnp.concatenate(pieces + pieces[:-1], axis=dim)
    return lax.dynamic_slice_in_dim(laid, first, RING * block.shape[dim], dim)


def ring_pieces(blocks, axes, half):
    ahead = [fetch(b, a, 1) for b, a in zip(blocks, axes)]
    behind = [fetch(b, a, 3) for b, a in zip(blocks, axes)]
    ahead, behind = lax.optimization_barrier((ahead, behind))
    size = blocks[0].shape[half] // 2
    first = [fetch(lax.slice_in_dim(v, 0, size, axis=half), a, 1) for v, a in zip(ahead, axes)]
    second = [fetch(lax.slice_in_dim(v, size, 2 * size, axis=half), a, 3) for v, a in zip(behind, axes)]
    return list(zip(ahead, first, second, behind))


def chunk(value, starts, step):
    return lax.dynamic_slice_in_dim(value, starts[step], value.shape[0] // RING, 0)


def coded(rows):
    top = jnp.max(jnp.abs(rows), axis=1, keepdims=True)
    scale = jnp.clip(jnp.floor(8.0 * jnp.log2(32000.0 / top)), -960.0, 960.0)
    body = jnp.round(rows * jnp.exp2(scale * 0.125)).astype(jnp.int16)
    tag = jnp.broadcast_to(scale, (rows.shape[0], 128)).astype(jnp.int16)
    return jnp.concatenate([body, tag], axis=1)


def decoded(sent):
    width = sent.shape[1] - 128
    scale = sent[:, width : width + 1].astype(f32)
    return sent[:, :width].astype(f32) * jnp.exp2(scale * -0.125)


def add_coded(near, received):
    rows, width = near[0].shape
    size = rows // 4

    def kernel(*refs):
        outs = refs[3 * len(near) :]
        for i in range(len(near)):
            value, arrived = refs[i], refs[len(near) + 2 * i : len(near) + 2 * i + 2]
            for k in range(4):
                block = value[k * size : (k + 1) * size, :]
                if k in (0, 3):
                    sent = arrived[k // 3]
                    scale = sent[:, width:].astype(jnp.int32).astype(f32)[:, :1]
                    block += sent[:, :width].astype(jnp.int32).astype(f32) * jnp.exp2(scale * -0.125)
                top = jnp.maximum(jnp.max(jnp.abs(block), axis=1, keepdims=True), 1e-30)
                scale = jnp.clip(jnp.floor(8.0 * jnp.log2(32000.0 / top)), -960.0, 960.0)
                body = jnp.round(block * jnp.exp2(scale * 0.125))
                out, at = outs[2 * i + k // 2], pl.ds(k % 2 * size, size)
                out[at, :width] = body.astype(jnp.int32).astype(jnp.int16)
                out[at, width:] = jnp.broadcast_to(scale, (size, 128)).astype(jnp.int32).astype(jnp.int16)

    vmem = pl.BlockSpec(memory_space=pltpu.VMEM)
    flat = [v for pair in received for v in pair]
    return pl.pallas_call(
        kernel,
        out_shape=[jax.ShapeDtypeStruct((2 * size, width + 128), jnp.int16)] * (2 * len(near)),
        in_specs=[vmem] * (3 * len(near)),
        out_specs=[vmem] * (2 * len(near)),
        compiler_params=pltpu.CompilerParams(vmem_limit_bytes=VMEM),
        name="add_coded",
    )(*near, *flat)


def scatter_direct(values, axes, places):
    sent = [coded(v) for v in values]
    got = [
        [fetch(chunk(v, p, (RING - d) % RING), a, d) for d in (1, 2, 3)] for v, a, p in zip(sent, axes, places)
    ]
    return [
        chunk(v, p, 0) + decoded(g[0]) + decoded(g[1]) + decoded(g[2]) for v, p, g in zip(values, places, got)
    ]


def scatter_ring(far, near, axes, later):
    size = far[0].shape[0] // 2
    far = [coded(v) for v in far]
    from_behind = [fetch(v[:size], a, 3) for v, a in zip(far, axes)]
    from_ahead = [fetch(v[size:], a, 1) for v, a in zip(far, axes)]
    flat = add_coded(near, list(zip(from_behind, from_ahead)))
    sent = list(zip(flat[0::2], flat[1::2]))
    sent, later = lax.optimization_barrier((sent, later))
    return [(decoded(fetch(f, a, 3)), decoded(fetch(b, a, 1))) for (f, b), a in zip(sent, axes)], later


def merge(stats, last=None):
    def pairwise(terms):
        if len(terms) == 2:
            return terms[0] + terms[1]
        return (terms[0] + terms[2]) + (terms[1] + terms[3])

    def top(terms):
        best = terms[0]
        for t in terms[1:]:
            best = jnp.maximum(best, t)
        return best

    def kernel(*refs):
        stat_refs, out = refs[: len(stats)], refs[-1]
        t_max, t_sum, s_max, s_sum, gap = ([ref[i : i + 1, :] for ref in stat_refs] for i in range(5))
        t_top, s_top = top(t_max), top(s_max)
        t_scale = [jnp.exp(m - t_top) for m in t_max]
        s_scale = [jnp.exp(m - s_top) for m in s_max]
        t_all = pairwise([a * b for a, b in zip(t_sum, t_scale)])
        s_all = pairwise([a * b for a, b in zip(s_sum, s_scale)])
        gap = pairwise([a * b for a, b in zip(gap, t_scale)])
        rows = [t_top, t_all, s_top, s_all, gap]
        if last:
            local, mask = refs[len(stats)], refs[len(stats) + 1][...]
            rows = [
                loss_scale * mask * jnp.exp(local[0:1, :] - t_top) / t_all,
                loss_scale * mask * jnp.exp(local[2:3, :] - s_top) / s_all,
                mask * (gap / t_all - t_top - jnp.log(t_all) + s_top + jnp.log(s_all)),
            ]
        out[...] = jnp.zeros_like(out)
        for i, row in enumerate(rows):
            out[i : i + 1, :] = row

    operands = [*stats, *(last or ())]
    vmem = pl.BlockSpec(memory_space=pltpu.VMEM)
    return pl.pallas_call(
        kernel,
        out_shape=jax.ShapeDtypeStruct(stats[0].shape, f32),
        in_specs=[vmem] * len(operands),
        out_specs=vmem,
        compiler_params=pltpu.CompilerParams(vmem_limit_bytes=4 * 1024 * 1024),
        name="merge",
    )(*operands)


def times(rows, head):
    return jnp.dot(rows, head, preferred_element_type=f32)


def softmax_rows(place, own, other, part):
    cols = own[0].shape[2]
    inner = 2 * part
    total = RING * RING * inner

    def kernel(place_ref, o_own, o_near, o_far, p_own, p_near, p_far, t_exp, s_exp, stats_ref, table):
        y, z = place_ref[0], place_ref[1]
        lane = lax.broadcasted_iota(jnp.int32, (inner, 128), 1)

        def logit(which, piece, at):
            o, p, base = {
                0: (o_own, p_own, 0),
                1: (o_near, p_near, 0),
                3: (o_near, p_near, RING * inner),
                2: (o_far, p_far, 0),
            }[piece]
            rows = pl.ds(base + at * inner, inner)
            return o[which, rows, :] + p[which, rows, :]

        for dz in range(RING):
            for dy in range(RING):
                t, s = logit(0, dz, dy), logit(1, dy, dz)
                t_max = jnp.max(t, axis=1, keepdims=True)
                s_max = jnp.max(s, axis=1, keepdims=True)
                te, se = jnp.exp(t - t_max), jnp.exp(s - s_max)
                values = [
                    t_max,
                    jnp.sum(te, axis=1, keepdims=True),
                    s_max,
                    jnp.sum(se, axis=1, keepdims=True),
                    jnp.sum(te * (t - s), axis=1, keepdims=True),
                ]
                row = jnp.zeros((inner, 128), f32)
                for i, v in enumerate(values):
                    row = jnp.where(lane == i, v, row)
                ya, za = lax.rem(y + dy, RING), lax.rem(z + dz, RING)
                first = pl.multiple_of((za * RING + ya) * part, 8)
                second = pl.multiple_of(total // 2 + (ya * RING + za) * part, 8)
                for at, lo in ((first, 0), (second, part)):
                    t_exp[pl.ds(at, part), :] = te[lo : lo + part]
                    s_exp[pl.ds(at, part), :] = se[lo : lo + part]
                    table[pl.ds(at, part), :] = row[lo : lo + part]
        stats_ref[...] = jnp.transpose(table[...])[:8]

    vmem = pl.BlockSpec(memory_space=pltpu.VMEM)
    return pl.pallas_call(
        kernel,
        out_shape=(
            jax.ShapeDtypeStruct((total, cols), f32),
            jax.ShapeDtypeStruct((total, cols), f32),
            jax.ShapeDtypeStruct((8, total), f32),
        ),
        in_specs=[pl.BlockSpec(memory_space=pltpu.SMEM)] + [vmem] * 6,
        out_specs=(vmem, vmem, vmem),
        scratch_shapes=[pltpu.VMEM((total, 128), f32)],
        compiler_params=pltpu.CompilerParams(vmem_limit_bytes=VMEM),
        name="softmax_rows",
    )(place, *own, *other)


def split_grad(place, t_exp, s_exp, factors):
    total, cols = t_exp.shape
    rows = total // 2 // RING

    def kernel(place_ref, t_ref, s_ref, factor_ref, own, near_z, near_y, far, table):
        y, z = place_ref[0], place_ref[1]
        table[...] = jnp.transpose(jnp.concatenate([factor_ref[...], jnp.zeros((120, total), f32)]))
        for half, at, near in ((0, z, near_z), (1, y, near_y)):
            for step, out, slot in ((0, own, half), (1, near, 0), (2, far, half), (3, near, 1)):
                here = pl.multiple_of(half * (total // 2) + lax.rem(at + step, RING) * rows, 8)
                scale = table[pl.ds(here, rows), :]
                grad = s_ref[pl.ds(here, rows), :] * scale[:, 1:2] - t_ref[pl.ds(here, rows), :] * scale[:, 0:1]
                high = grad.astype(bf16)
                low = (grad - high.astype(f32)).astype(bf16)
                to = slot * rows
                out[0, to : to + rows, :] = high
                out[1, to : to + rows, :] = low

    vmem = pl.BlockSpec(memory_space=pltpu.VMEM)
    shape = jax.ShapeDtypeStruct((2, 2 * rows, cols), bf16)
    return pl.pallas_call(
        kernel,
        out_shape=(shape,) * 4,
        in_specs=[pl.BlockSpec(memory_space=pltpu.SMEM)] + [vmem] * 3,
        out_specs=(vmem,) * 4,
        scratch_shapes=[pltpu.VMEM((total, 128), f32)],
        compiler_params=pltpu.CompilerParams(vmem_limit_bytes=VMEM),
        name="split_grad",
    )(place, t_exp, s_exp, factors)


def chunk_grad(own, par, own_head, par_head):
    _, rows, cols = own.shape
    dims = (((1,), (1,)), ((), ()))
    both = lax.dot_general(own.reshape(2 * rows, cols), own_head, dims, preferred_element_type=f32)
    both += lax.dot_general(par.reshape(2 * rows, cols), par_head, dims, preferred_element_type=f32)
    return both[:rows] + both[rows:]


def shards(
    teacher_hidden, teacher_target, student_hidden, tile_count, response_mask, teacher_head, student_head
):
    n_seq = lax.axis_size("seq")
    features = teacher_hidden.shape[1]
    share = TILE // n_seq
    seq, voc = lax.axis_index("seq"), lax.axis_index("vocab")
    y, z, x, c = seq // RING, seq % RING, voc // 2, voc % 2
    part = LIVE // 2 * share
    parity = c.astype(jnp.uint32)
    place = jnp.stack([y, z]).astype(jnp.int32)
    starts = {
        axis: [((at + d) % RING * size).astype(jnp.uint32) for d in range(RING)]
        for axis, at, size in (("y", y, part), ("z", z, part), ("x", x, 2 * part))
    }
    first_x = ((RING - x) % RING * features).astype(jnp.uint32)

    rows = jnp.concatenate(
        [teacher_hidden.reshape(n_seq, share, features), student_hidden.reshape(n_seq, share, features)], axis=1
    )
    lists = jnp.concatenate(
        [
            response_mask.astype(bf16)[None],
            jnp.broadcast_to(teacher_target.astype(bf16)[:, None], (1, TILE)),
            jnp.broadcast_to(tile_count.astype(bf16)[:, None], (1, TILE)),
            jnp.zeros((2 * share - 3, TILE), bf16),
        ]
    )
    sent = jnp.concatenate([rows, jnp.broadcast_to(lists[None], (n_seq, 2 * share, TILE))], axis=2)
    sent, parity, place, starts, first_x = lax.optimization_barrier((sent, parity, place, starts, first_x))
    got = lax.all_to_all(sent, "seq", 0, 0, tiled=True)

    def half(head, which):
        blocks = head.reshape(RING, 2, features, -1)
        return lax.dynamic_index_in_dim(blocks, which, 1, keepdims=False).reshape(RING * features, -1)

    kept, given = ([half(h, i) for h in (teacher_head, student_head)] for i in (parity, 1 - parity))
    got, kept, given = lax.optimization_barrier((got, kept, given))
    t_head, s_head = kept
    all_mask = got[:, 0, features:].astype(f32)
    all_target = got[:, 1, features].astype(jnp.int32)
    all_count = got[:, 2, features].astype(jnp.int32)
    slot_ids = jnp.arange(LIVE, dtype=jnp.int32)
    tiles = jnp.arange(n_seq, dtype=jnp.int32)
    before = jnp.sum(jnp.where(tiles[None, :] < tiles[:, None], all_count[None, :], 0), axis=1)
    slot_of = jnp.where(all_count > 0, before, -1)
    t_match = all_target[None, :] == slot_ids[:, None]
    s_match = slot_of[None, :] == slot_ids[:, None]

    def pick(match, tiles):
        return jnp.sum(jnp.where(match[:, :, None, None], tiles[None].astype(f32), 0.0), axis=1).astype(bf16)

    t_rows = pick(t_match, got[:, :share, :features]).reshape(LIVE * share, features)
    s_rows = pick(s_match, got[:, share:, :features]).reshape(LIVE * share, features)
    mask = jnp.sum(jnp.where(s_match[:, :, None], all_mask[None], 0.0), axis=1)
    masked_count = jnp.sum(mask)
    row = lax.broadcasted_iota(jnp.int32, (TILE, LIVE * TILE), 0)
    col = lax.broadcasted_iota(jnp.int32, (TILE, LIVE * TILE), 1)
    outer, inner = col % (LIVE // 2 * TILE) // (RING * part), col % (RING * part) // part
    second = col >= LIVE // 2 * TILE
    wanted = jnp.where(second, outer * RING + inner, inner * RING + outer) * share + col % share
    spread = jnp.dot(mask.astype(bf16), (row == wanted).astype(bf16), preferred_element_type=f32)
    tile = (col % part // share + jnp.where(second, LIVE // 2, 0))[:LIVE]
    row_mask = jnp.sum(jnp.where(tile == row[:LIVE], spread, 0.0), axis=0, keepdims=True)
    t_par, s_par = (fetch(g, "c", 1) for g in given)

    block = gather_direct(jnp.stack([t_rows, s_rows]), "x", first_x, 2)
    block, t_par, s_par = lax.optimization_barrier((block, t_par, s_par))
    t_block, s_block = block[0], block[1]

    t_ring, s_ring = ring_pieces((t_block, s_block), ("y", "z"), 1)

    def stacked(rows, ring):
        ahead, first, second, behind = ring
        return jnp.concatenate([rows, ahead, jnp.concatenate([first, second], axis=1), behind], axis=0)

    t_own, s_own = stacked(t_block, t_ring), stacked(s_block, s_ring)
    t_own, s_own = lax.optimization_barrier((t_own, s_own))
    t_ring, s_ring = ring_pieces((t_own, s_own), ("z", "y"), 0)
    t_near, s_near = (jnp.concatenate([r[0], r[3]]) for r in (t_ring, s_ring))
    t_far, s_far = (jnp.concatenate([r[1], r[2]]) for r in (t_ring, s_ring))
    both = lambda t, s: jnp.concatenate([t[None], s[None]])
    other_own, other_near = both(times(t_own, t_par), times(s_own, s_par)), both(times(t_near, t_par), times(s_near, s_par))
    mine_own, mine_near = both(times(t_own, t_head), times(s_own, s_head)), both(times(t_near, t_head), times(s_near, s_head))
    other_own, other_near = fetch(other_own, "c", 1), fetch(other_near, "c", 1)
    t_far, s_far, mine_own, mine_near = lax.optimization_barrier((t_far, s_far, mine_own, mine_near))
    other_far = fetch(both(times(t_far, t_par), times(s_far, s_par)), "c", 1)
    mine_far = both(times(t_far, t_head), times(s_far, s_head))
    mine, other = (mine_own, mine_near, mine_far), (other_own, other_near, other_far)
    t_exp, s_exp, local = softmax_rows(place, mine, other, part)

    stats = merge([local, fetch(local, "c", 1)])
    for axis in ("x", "y", "z"):
        stats = merge(
            [stats] + [fetch(stats, axis, d) for d in (1, 2, 3)], (local, row_mask) if axis == "z" else None
        )
    factors = stats
    mean_loss = jnp.sum(stats[2]) / masked_count
    own, near_z, near_y, far = split_grad(place, t_exp, s_exp, factors)

    far_par, near_z_par, near_y_par, own_par = (fetch(v, "c", 1) for v in (far, near_z, near_y, own))
    rows = RING * part
    far = chunk_grad(far, far_par, s_head, s_par)
    near_z, near_z_par, near_y, near_y_par, far = lax.optimization_barrier((near_z, near_z_par, near_y, near_y_par, far))
    near_z = chunk_grad(near_z, near_z_par, s_head, s_par)
    near_y = chunk_grad(near_y, near_y_par, s_head, s_par)
    cut = lambda v: [v[:rows], v[rows:]]
    got, later = scatter_ring(cut(far), [near_z, near_y], ("z", "y"), (own, own_par))
    own = cut(chunk_grad(*later, s_head, s_par))
    summed = [o + a + b for o, (a, b) in zip(own, got)]
    summed = jnp.concatenate(scatter_direct(summed, ("y", "z"), (starts["y"], starts["z"])))
    summed = summed.reshape(LIVE * share, RING, features).transpose(1, 0, 2).reshape(RING * LIVE * share, features)
    (summed,) = scatter_direct([summed], ["x"], [starts["x"]])
    summed = summed.reshape(LIVE, share, features)
    back = jnp.sum(jnp.where(s_match[:, :, None, None], summed[:, None], 0.0), axis=0)
    own_rows = lax.all_to_all(back, "seq", 0, 0, tiled=True)
    return mean_loss, own_rows.reshape(TILE, features)


def solution(mesh):
    return jax.shard_map(
        shards,
        mesh=mesh,
        in_specs=(
            P("seq", "vocab"),
            P("seq"),
            P("seq", "vocab"),
            P("seq"),
            P("seq"),
            P(None, BOTH),
            P(None, BOTH),
        ),
        out_specs=(P(), P("seq", "vocab")),
        check_vma=False,
    )
```

```python
import jax
import jax.numpy as jnp
from jax import lax
from jax.experimental import pallas as pl
from jax.experimental.pallas import tpu as pltpu
from jax.sharding import PartitionSpec as P

TILE = 128
LIVE = 6
RING = 4
BOTH = ("seq", "vocab")
loss_scale = 64.0
VMEM = 20 * 1024 * 1024
f32 = jnp.float32
bf16 = jnp.bfloat16


def device_of(y, z, x, c):
    return (y * RING + z) * 2 * RING + x * 2 + c


def fetch(value, axis, step):
    pairs = []
    for y in range(RING):
        for z in range(RING):
            for x in range(RING):
                for c in range(2):
                    at = dict(y=y, z=z, x=x, c=c)
                    here = device_of(**at)
                    at[axis] = (at[axis] + step) % (2 if axis == "c" else RING)
                    pairs.append((device_of(**at), here))
    return lax.ppermute(value, BOTH, pairs)


def gather_direct(block, axis, first, dim):
    pieces = [block] + [fetch(block, axis, d) for d in (1, 2, 3)]
    laid = jnp.concatenate(pieces + pieces[:-1], axis=dim)
    return lax.dynamic_slice_in_dim(laid, first, RING * block.shape[dim], dim)


def ring_pieces(blocks, axes, half):
    ahead = [fetch(b, a, 1) for b, a in zip(blocks, axes)]
    behind = [fetch(b, a, 3) for b, a in zip(blocks, axes)]
    ahead, behind = lax.optimization_barrier((ahead, behind))
    size = blocks[0].shape[half] // 2
    first = [fetch(lax.slice_in_dim(v, 0, size, axis=half), a, 1) for v, a in zip(ahead, axes)]
    second = [fetch(lax.slice_in_dim(v, size, 2 * size, axis=half), a, 3) for v, a in zip(behind, axes)]
    return list(zip(ahead, first, second, behind))


def chunk(value, starts, step):
    return lax.dynamic_slice_in_dim(value, starts[step], value.shape[0] // RING, 0)


def coded(rows):
    top = jnp.max(jnp.abs(rows), axis=1, keepdims=True)
    scale = jnp.clip(jnp.floor(8.0 * jnp.log2(32000.0 / top)), -960.0, 960.0)
    body = jnp.round(rows * jnp.exp2(scale * 0.125)).astype(jnp.int16)
    tag = jnp.broadcast_to(scale, (rows.shape[0], 128)).astype(jnp.int16)
    return jnp.concatenate([body, tag], axis=1)


def decoded(sent):
    width = sent.shape[1] - 128
    scale = sent[:, width : width + 1].astype(f32)
    return sent[:, :width].astype(f32) * jnp.exp2(scale * -0.125)


def add_coded(near, received):
    rows, width = near[0].shape
    size = rows // 4

    def kernel(*refs):
        outs = refs[3 * len(near) :]
        for i in range(len(near)):
            value, arrived = refs[i], refs[len(near) + 2 * i : len(near) + 2 * i + 2]
            for k in range(4):
                block = value[k * size : (k + 1) * size, :]
                if k in (0, 3):
                    sent = arrived[k // 3]
                    scale = sent[:, width:].astype(jnp.int32).astype(f32)[:, :1]
                    block += sent[:, :width].astype(jnp.int32).astype(f32) * jnp.exp2(scale * -0.125)
                top = jnp.maximum(jnp.max(jnp.abs(block), axis=1, keepdims=True), 1e-30)
                scale = jnp.clip(jnp.floor(8.0 * jnp.log2(32000.0 / top)), -960.0, 960.0)
                body = jnp.round(block * jnp.exp2(scale * 0.125))
                out, at = outs[2 * i + k // 2], pl.ds(k % 2 * size, size)
                out[at, :width] = body.astype(jnp.int32).astype(jnp.int16)
                out[at, width:] = jnp.broadcast_to(scale, (size, 128)).astype(jnp.int32).astype(jnp.int16)

    vmem = pl.BlockSpec(memory_space=pltpu.VMEM)
    flat = [v for pair in received for v in pair]
    return pl.pallas_call(
        kernel,
        out_shape=[jax.ShapeDtypeStruct((2 * size, width + 128), jnp.int16)] * (2 * len(near)),
        in_specs=[vmem] * (3 * len(near)),
        out_specs=[vmem] * (2 * len(near)),
        compiler_params=pltpu.CompilerParams(vmem_limit_bytes=VMEM),
        name="add_coded",
    )(*near, *flat)


def scatter_direct(values, axes, places):
    sent = [coded(v) for v in values]
    got = [
        [fetch(chunk(v, p, (RING - d) % RING), a, d) for d in (1, 2, 3)] for v, a, p in zip(sent, axes, places)
    ]
    return [
        chunk(v, p, 0) + decoded(g[0]) + decoded(g[1]) + decoded(g[2]) for v, p, g in zip(values, places, got)
    ]


def scatter_ring(far, near, axes, later):
    size = far[0].shape[0] // 2
    far = [coded(v) for v in far]
    from_behind = [fetch(v[:size], a, 3) for v, a in zip(far, axes)]
    from_ahead = [fetch(v[size:], a, 1) for v, a in zip(far, axes)]
    flat = add_coded(near, list(zip(from_behind, from_ahead)))
    sent = list(zip(flat[0::2], flat[1::2]))
    sent, later = lax.optimization_barrier((sent, later))
    return [(decoded(fetch(f, a, 3)), decoded(fetch(b, a, 1))) for (f, b), a in zip(sent, axes)], later


def merge(stats, last=None):
    def pairwise(terms):
        if len(terms) == 2:
            return terms[0] + terms[1]
        return (terms[0] + terms[2]) + (terms[1] + terms[3])

    def top(terms):
        best = terms[0]
        for t in terms[1:]:
            best = jnp.maximum(best, t)
        return best

    def kernel(*refs):
        stat_refs, out = refs[: len(stats)], refs[-1]
        t_max, t_sum, s_max, s_sum, gap = ([ref[i : i + 1, :] for ref in stat_refs] for i in range(5))
        t_top, s_top = top(t_max), top(s_max)
        t_scale = [jnp.exp(m - t_top) for m in t_max]
        s_scale = [jnp.exp(m - s_top) for m in s_max]
        t_all = pairwise([a * b for a, b in zip(t_sum, t_scale)])
        s_all = pairwise([a * b for a, b in zip(s_sum, s_scale)])
        gap = pairwise([a * b for a, b in zip(gap, t_scale)])
        rows = [t_top, t_all, s_top, s_all, gap]
        if last:
            local, mask = refs[len(stats)], refs[len(stats) + 1][...]
            rows = [
                loss_scale * mask * jnp.exp(local[0:1, :] - t_top) / t_all,
                loss_scale * mask * jnp.exp(local[2:3, :] - s_top) / s_all,
                mask * (gap / t_all - t_top - jnp.log(t_all) + s_top + jnp.log(s_all)),
            ]
        out[...] = jnp.zeros_like(out)
        for i, row in enumerate(rows):
            out[i : i + 1, :] = row

    operands = [*stats, *(last or ())]
    vmem = pl.BlockSpec(memory_space=pltpu.VMEM)
    return pl.pallas_call(
        kernel,
        out_shape=jax.ShapeDtypeStruct(stats[0].shape, f32),
        in_specs=[vmem] * len(operands),
        out_specs=vmem,
        compiler_params=pltpu.CompilerParams(vmem_limit_bytes=4 * 1024 * 1024),
        name="merge",
    )(*operands)


def times(rows, head):
    return jnp.dot(rows, head, preferred_element_type=f32)


def softmax_rows(place, own, other, part):
    cols = own[0].shape[2]
    inner = 2 * part
    total = RING * RING * inner

    def kernel(place_ref, o_own, o_near, o_far, p_own, p_near, p_far, t_exp, s_exp, stats_ref, table):
        y, z = place_ref[0], place_ref[1]
        lane = lax.broadcasted_iota(jnp.int32, (inner, 128), 1)

        def logit(which, piece, at):
            o, p, base = {
                0: (o_own, p_own, 0),
                1: (o_near, p_near, 0),
                3: (o_near, p_near, RING * inner),
                2: (o_far, p_far, 0),
            }[piece]
            rows = pl.ds(base + at * inner, inner)
            return o[which, rows, :] + p[which, rows, :]

        for dz in range(RING):
            for dy in range(RING):
                t, s = logit(0, dz, dy), logit(1, dy, dz)
                t_max = jnp.max(t, axis=1, keepdims=True)
                s_max = jnp.max(s, axis=1, keepdims=True)
                te, se = jnp.exp(t - t_max), jnp.exp(s - s_max)
                values = [
                    t_max,
                    jnp.sum(te, axis=1, keepdims=True),
                    s_max,
                    jnp.sum(se, axis=1, keepdims=True),
                    jnp.sum(te * (t - s), axis=1, keepdims=True),
                ]
                row = jnp.zeros((inner, 128), f32)
                for i, v in enumerate(values):
                    row = jnp.where(lane == i, v, row)
                ya, za = lax.rem(y + dy, RING), lax.rem(z + dz, RING)
                first = pl.multiple_of((za * RING + ya) * part, 8)
                second = pl.multiple_of(total // 2 + (ya * RING + za) * part, 8)
                for at, lo in ((first, 0), (second, part)):
                    t_exp[pl.ds(at, part), :] = te[lo : lo + part]
                    s_exp[pl.ds(at, part), :] = se[lo : lo + part]
                    table[pl.ds(at, part), :] = row[lo : lo + part]
        stats_ref[...] = jnp.transpose(table[...])[:8]

    vmem = pl.BlockSpec(memory_space=pltpu.VMEM)
    return pl.pallas_call(
        kernel,
        out_shape=(
            jax.ShapeDtypeStruct((total, cols), f32),
            jax.ShapeDtypeStruct((total, cols), f32),
            jax.ShapeDtypeStruct((8, total), f32),
        ),
        in_specs=[pl.BlockSpec(memory_space=pltpu.SMEM)] + [vmem] * 6,
        out_specs=(vmem, vmem, vmem),
        scratch_shapes=[pltpu.VMEM((total, 128), f32)],
        compiler_params=pltpu.CompilerParams(vmem_limit_bytes=VMEM),
        name="softmax_rows",
    )(place, *own, *other)


def split_grad(place, t_exp, s_exp, factors):
    total, cols = t_exp.shape
    rows = total // 2 // RING

    def kernel(place_ref, t_ref, s_ref, factor_ref, own, near_z, near_y, far, table):
        y, z = place_ref[0], place_ref[1]
        table[...] = jnp.transpose(jnp.concatenate([factor_ref[...], jnp.zeros((120, total), f32)]))
        for half, at, near in ((0, z, near_z), (1, y, near_y)):
            for step, out, slot in ((0, own, half), (1, near, 0), (2, far, half), (3, near, 1)):
                here = pl.multiple_of(half * (total // 2) + lax.rem(at + step, RING) * rows, 8)
                scale = table[pl.ds(here, rows), :]
                grad = s_ref[pl.ds(here, rows), :] * scale[:, 1:2] - t_ref[pl.ds(here, rows), :] * scale[:, 0:1]
                high = grad.astype(bf16)
                low = (grad - high.astype(f32)).astype(bf16)
                to = slot * rows
                out[0, to : to + rows, :] = high
                out[1, to : to + rows, :] = low

    vmem = pl.BlockSpec(memory_space=pltpu.VMEM)
    shape = jax.ShapeDtypeStruct((2, 2 * rows, cols), bf16)
    return pl.pallas_call(
        kernel,
        out_shape=(shape,) * 4,
        in_specs=[pl.BlockSpec(memory_space=pltpu.SMEM)] + [vmem] * 3,
        out_specs=(vmem,) * 4,
        scratch_shapes=[pltpu.VMEM((total, 128), f32)],
        compiler_params=pltpu.CompilerParams(vmem_limit_bytes=VMEM),
        name="split_grad",
    )(place, t_exp, s_exp, factors)


def chunk_grad(own, par, own_head, par_head):
    _, rows, cols = own.shape
    dims = (((1,), (1,)), ((), ()))
    both = lax.dot_general(own.reshape(2 * rows, cols), own_head, dims, preferred_element_type=f32)
    both += lax.dot_general(par.reshape(2 * rows, cols), par_head, dims, preferred_element_type=f32)
    return both[:rows] + both[rows:]


def shards(
    teacher_hidden, teacher_target, student_hidden, tile_count, response_mask, teacher_head, student_head
):
    n_seq = lax.axis_size("seq")
    features = teacher_hidden.shape[1]
    share = TILE // n_seq
    seq, voc = lax.axis_index("seq"), lax.axis_index("vocab")
    y, z, x, c = seq // RING, seq % RING, voc // 2, voc % 2
    part = LIVE // 2 * share
    parity = c.astype(jnp.uint32)
    place = jnp.stack([y, z]).astype(jnp.int32)
    starts = {
        axis: [((at + d) % RING * size).astype(jnp.uint32) for d in range(RING)]
        for axis, at, size in (("y", y, part), ("z", z, part), ("x", x, 2 * part))
    }
    first_x = ((RING - x) % RING * features).astype(jnp.uint32)

    rows = jnp.concatenate(
        [teacher_hidden.reshape(n_seq, share, features), student_hidden.reshape(n_seq, share, features)], axis=1
    )
    lists = jnp.concatenate(
        [
            response_mask.astype(bf16)[None],
            jnp.broadcast_to(teacher_target.astype(bf16)[:, None], (1, TILE)),
            jnp.broadcast_to(tile_count.astype(bf16)[:, None], (1, TILE)),
            jnp.zeros((2 * share - 3, TILE), bf16),
        ]
    )
    sent = jnp.concatenate([rows, jnp.broadcast_to(lists[None], (n_seq, 2 * share, TILE))], axis=2)
    sent, parity, place, starts, first_x = lax.optimization_barrier((sent, parity, place, starts, first_x))
    got = lax.all_to_all(sent, "seq", 0, 0, tiled=True)

    def half(head, which):
        blocks = head.reshape(RING, 2, features, -1)
        return lax.dynamic_index_in_dim(blocks, which, 1, keepdims=False).reshape(RING * features, -1)

    kept, given = ([half(h, i) for h in (teacher_head, student_head)] for i in (parity, 1 - parity))
    got, kept, given = lax.optimization_barrier((got, kept, given))
    t_head, s_head = kept
    all_mask = got[:, 0, features:].astype(f32)
    all_target = got[:, 1, features].astype(jnp.int32)
    all_count = got[:, 2, features].astype(jnp.int32)
    slot_ids = jnp.arange(LIVE, dtype=jnp.int32)
    tiles = jnp.arange(n_seq, dtype=jnp.int32)
    before = jnp.sum(jnp.where(tiles[None, :] < tiles[:, None], all_count[None, :], 0), axis=1)
    slot_of = jnp.where(all_count > 0, before, -1)
    t_match = all_target[None, :] == slot_ids[:, None]
    s_match = slot_of[None, :] == slot_ids[:, None]

    def pick(match, tiles):
        return jnp.sum(jnp.where(match[:, :, None, None], tiles[None].astype(f32), 0.0), axis=1).astype(bf16)

    t_rows = pick(t_match, got[:, :share, :features]).reshape(LIVE * share, features)
    s_rows = pick(s_match, got[:, share:, :features]).reshape(LIVE * share, features)
    mask = jnp.sum(jnp.where(s_match[:, :, None], all_mask[None], 0.0), axis=1)
    masked_count = jnp.sum(mask)
    row = lax.broadcasted_iota(jnp.int32, (TILE, LIVE * TILE), 0)
    col = lax.broadcasted_iota(jnp.int32, (TILE, LIVE * TILE), 1)
    outer, inner = col % (LIVE // 2 * TILE) // (RING * part), col % (RING * part) // part
    second = col >= LIVE // 2 * TILE
    wanted = jnp.where(second, outer * RING + inner, inner * RING + outer) * share + col % share
    spread = jnp.dot(mask.astype(bf16), (row == wanted).astype(bf16), preferred_element_type=f32)
    tile = (col % part // share + jnp.where(second, LIVE // 2, 0))[:LIVE]
    row_mask = jnp.sum(jnp.where(tile == row[:LIVE], spread, 0.0), axis=0, keepdims=True)
    t_par, s_par = (fetch(g, "c", 1) for g in given)

    block = gather_direct(jnp.stack([t_rows, s_rows]), "x", first_x, 2)
    block, t_par, s_par = lax.optimization_barrier((block, t_par, s_par))
    t_block, s_block = block[0], block[1]

    t_ring, s_ring = ring_pieces((t_block, s_block), ("y", "z"), 1)

    def stacked(rows, ring):
        ahead, first, second, behind = ring
        return jnp.concatenate([rows, ahead, jnp.concatenate([first, second], axis=1), behind], axis=0)

    t_own, s_own = stacked(t_block, t_ring), stacked(s_block, s_ring)
    t_own, s_own = lax.optimization_barrier((t_own, s_own))
    t_ring, s_ring = ring_pieces((t_own, s_own), ("z", "y"), 0)
    t_near, s_near = (jnp.concatenate([r[0], r[3]]) for r in (t_ring, s_ring))
    t_far, s_far = (jnp.concatenate([r[1], r[2]]) for r in (t_ring, s_ring))
    both = lambda t, s: jnp.concatenate([t[None], s[None]])
    other_own, other_near = both(times(t_own, t_par), times(s_own, s_par)), both(times(t_near, t_par), times(s_near, s_par))
    mine_own, mine_near = both(times(t_own, t_head), times(s_own, s_head)), both(times(t_near, t_head), times(s_near, s_head))
    other_own, other_near = fetch(other_own, "c", 1), fetch(other_near, "c", 1)
    t_far, s_far, mine_own = lax.optimization_barrier((t_far, s_far, mine_own))
    other_far = fetch(both(times(t_far, t_par), times(s_far, s_par)), "c", 1)
    mine_far = both(times(t_far, t_head), times(s_far, s_head))
    mine, other = (mine_own, mine_near, mine_far), (other_own, other_near, other_far)
    t_exp, s_exp, local = softmax_rows(place, mine, other, part)

    stats = merge([local, fetch(local, "c", 1)])
    for axis in ("x", "y", "z"):
        stats = merge(
            [stats] + [fetch(stats, axis, d) for d in (1, 2, 3)], (local, row_mask) if axis == "z" else None
        )
    factors = stats
    mean_loss = jnp.sum(stats[2]) / masked_count
    own, near_z, near_y, far = split_grad(place, t_exp, s_exp, factors)

    far_par, near_z_par, near_y_par, own_par = (fetch(v, "c", 1) for v in (far, near_z, near_y, own))
    rows = RING * part
    far = chunk_grad(far, far_par, s_head, s_par)
    near_z, near_z_par, near_y, near_y_par, far = lax.optimization_barrier((near_z, near_z_par, near_y, near_y_par, far))
    near_z = chunk_grad(near_z, near_z_par, s_head, s_par)
    near_y = chunk_grad(near_y, near_y_par, s_head, s_par)
    cut = lambda v: [v[:rows], v[rows:]]
    got, later = scatter_ring(cut(far), [near_z, near_y], ("z", "y"), (own, own_par))
    own = cut(chunk_grad(*later, s_head, s_par))
    summed = [o + a + b for o, (a, b) in zip(own, got)]
    summed = jnp.concatenate(scatter_direct(summed, ("y", "z"), (starts["y"], starts["z"])))
    summed = summed.reshape(LIVE * share, RING, features).transpose(1, 0, 2).reshape(RING * LIVE * share, features)
    (summed,) = scatter_direct([summed], ["x"], [starts["x"]])
    summed = summed.reshape(LIVE, share, features)
    back = jnp.sum(jnp.where(s_match[:, :, None, None], summed[:, None], 0.0), axis=0)
    own_rows = lax.all_to_all(back, "seq", 0, 0, tiled=True)
    return mean_loss, own_rows.reshape(TILE, features)


def solution(mesh):
    return jax.shard_map(
        shards,
        mesh=mesh,
        in_specs=(
            P("seq", "vocab"),
            P("seq"),
            P("seq", "vocab"),
            P("seq"),
            P("seq"),
            P(None, BOTH),
            P(None, BOTH),
        ),
        out_specs=(P(), P("seq", "vocab")),
        check_vma=False,
    )
```
